32 devices in a mesh: sec: 2 (over y), row: 4 (over x, core), col: 4 (over z).
Axes of the slice: x: 2, y: 2, z: 4, core: 2. Of those that a mesh axis runs over, the one named last changes fastest.
Arguments:
- sketch: float32 [32, 64, 2048], P(None, ('sec', 'row'), 'col'), parts along dimension 1, may hold values from -6 to 6
- weights: float32 [8, 64, 2048], P(None, ('sec', 'row'), 'col'), parts along dimension 1, may hold values from 0.05 to 1
Outputs:
- basis: float32 [32, 64, 2048], P(None, ('sec', 'row'), 'col'), parts along dimension 1
- factor: float32 [64, 32], P('sec'), parts along dimension 0
The draws below stay inside these ranges and needn't reach their ends.
There are 2 independent parts, one for each index of `sec`. The reference program is written for one: setup_inputs(seed, part) draws one part's arguments, and reference() takes and returns one part's arrays. A program takes and returns all parts, laid end to end along the dimension named above; each array names one. Nothing has to cross between parts.
All inputs are finite; a program needn't handle non-finite values.
Results may differ from the reference program's by a relative error of at most 0.0001.
Values sent between devices are 32-bit elements; how exact they have to be, the bound alone decides.
A program may use at most 64 MiB of HBM per device.

```python
import math
import jax
import jax.numpy as jnp
from jax import lax

K = 32
ITERS = 2
H = 32
W = 2048


def steps_of(stream_key, extent, split, low, largest):
    gain, own = 1.0, jax.random.fold_in(stream_key, 6)
    for axis_at, parts in split:
        steps = jnp.exp(jax.random.uniform(jax.random.fold_in(own, axis_at), (parts,), jnp.float32, low / len(split), largest / len(split)))
        gain = gain * jnp.repeat(steps, extent[axis_at] // parts).reshape([-1 if axis == axis_at else 1 for axis in range(len(extent))])
    return gain


def scatter_about(stream_key, dims, width, bound, shards=(), kind=jnp.bfloat16):
    result = width * jax.random.normal(stream_key, dims, jnp.float32)
    if shards:
        result = result * steps_of(stream_key, dims, shards, -0.22, 0.18)
    return jnp.clip(result, -bound, bound).astype(kind)


def setup_inputs(seed: int = 0, part: int = 0) -> dict:
    key_of = jax.random.split(jax.random.key(seed), 3)
    part_splits = jax.random.split(jax.random.fold_in(key_of[2], part), 3)
    return {
        "sketch": scatter_about(part_splits[0], (K, H, W), 1.0, 6.0, ((1, 4), (2, 4)), jnp.float32),
        "weights": jnp.clip(jnp.exp(math.log(1.0) - 2.9957323 * jax.random.uniform(part_splits[1], (8, H, W), jnp.float32) ** steps_of(part_splits[1], (8, H, W), ((1, 4), (2, 4)), -0.2, 0.2)), 0.05, 1.0),
    }


NEIGHBOURS = ((-1, -1), (-1, 0), (-1, 1), (0, -1), (0, 1), (1, -1), (1, 0), (1, 1))

def operate(planes, weights):
    height = planes.shape[1]
    breadth = planes.shape[2]
    padded = jnp.pad(planes, ((0, 0), (1, 1), (1, 1)))
    summed = jnp.sum(weights, axis=0) * planes
    for position, offset in enumerate(NEIGHBOURS):
        shift_row = offset[0]
        shift_col = offset[1]
        summed = summed + weights[position] * padded[:, 1 + shift_row:1 + shift_row + height, 1 + shift_col:1 + shift_col + breadth]
    return summed

def reference(sketch, weights):
    sketch_field = sketch
    lower_tri = jnp.zeros((K, K), jnp.float32)
    for power_step in range(ITERS):
        blocks = sketch_field.reshape(K // 8, 8, H, W)
        image_vals = lax.map(lambda block: operate(block, weights), blocks).reshape(K, H * W)
        gram_full = jnp.dot(image_vals, image_vals.T, precision=lax.Precision.HIGHEST) / (H * W)
        lower_tri = jnp.linalg.cholesky(gram_full)
        solved = jax.scipy.linalg.solve_triangular(lower_tri, image_vals, lower=True)
        sketch_field = solved.reshape(K, H, W)
    return (sketch_field, lower_tri.T)
```

```python
import functools

import jax
import jax.numpy as jnp
from jax import lax
from jax.experimental import pallas as pl
from jax.experimental.pallas import tpu as pltpu
from jax.sharding import PartitionSpec as P

LANES = 128
SUB = 8
MESH = pl.DeviceIdType.MESH
NT = (((1,), (1,)), ((), ()))
HIGHEST = lax.Precision.HIGHEST
f32 = jnp.float32
bf16 = jnp.bfloat16


def split(x):
    hi = x.astype(bf16)
    lo = (x - hi.astype(f32)).astype(bf16)
    return hi, lo


def kernel(
    n, rows, cols, R, C, stages, rounds,
    sk_hbm, w_hbm, y2_out, tables,
    raw, wraw, x, w, ws, y1, y2, pack, nb, held, sent,
    load_sem, col_send, col_recv, row_send, row_recv, gather_send, gather_recv, reach,
):
    groups = n // SUB
    tiles = cols // LANES
    i = lax.axis_index("row")
    j = lax.axis_index("col")
    has_up, has_down = i > 0, i < R - 1
    has_left, has_right = j > 0, j < C - 1

    def cond(*terms):
        terms = [t for t in terms if t is not None]
        return functools.reduce(jnp.logical_and, terms)

    ups = {-1: has_up, 0: None, 1: has_down}
    sides = {-1: has_left, 0: None, 1: has_right}
    around = [(dr, dc) for dr in (0, -1, 1) for dc in (-1, 1)] + [(-1, 0), (1, 0)]

    def at_offset(dr, dc):
        return {"row": i + dr, "col": j + dc}

    def greet(sem):
        for dr, dc in around:
            @pl.when(cond(ups[dr], sides[dc]))
            def _(dr=dr, dc=dc):
                pl.semaphore_signal(sem, inc=1, device_id=at_offset(dr, dc), device_id_type=MESH)

    height = 1 + has_up.astype(jnp.int32) + has_down.astype(jnp.int32)
    breadth = 1 + has_left.astype(jnp.int32) + has_right.astype(jnp.int32)
    neighbours = height * breadth - 1

    barrier = pltpu.get_barrier_semaphore()
    greet(barrier)

    loads = []
    for t in range(tiles):
        across = pl.ds(t * LANES, LANES)
        loads.append(pltpu.make_async_copy(sk_hbm.at[:, across], raw.at[t], load_sem.at[0, t]))
        loads.append(pltpu.make_async_copy(w_hbm.at[:, across], wraw.at[t], load_sem.at[1, t]))
    for load in loads:
        load.start()

    lane = lax.broadcasted_iota(jnp.int32, (SUB, LANES), 1)
    sub = lax.broadcasted_iota(jnp.int32, (SUB, LANES), 0)

    with jax.named_scope("load"):
        for load in loads:
            load.wait()
    with jax.named_scope("relayout"):
        for t in range(tiles):
            for r in range(rows):
                for g in range(groups):
                    x[t, r + 2, g * SUB : (g + 1) * SUB, :] = raw[
                        t, pl.ds(g * SUB * rows + r, SUB, stride=rows), :
                    ]
                w[t, r + 1] = wraw[t, pl.ds(r, SUB, stride=rows), :]

    outer = [0, 1, rows - 2, rows - 1]
    inner = list(range(2, rows - 2))
    halves = (outer, inner)

    with jax.named_scope("pack"):
        for h, members in enumerate(halves):
            packed = jnp.zeros((SUB, LANES), f32)
            for at, r in enumerate(members):
                for g in range(groups + 1):
                    if g < groups:
                        slot = at * groups + g
                        first = x[0, r + 2, g * SUB : (g + 1) * SUB, :]
                        final = x[tiles - 1, r + 2, g * SUB : (g + 1) * SUB, :]
                    else:
                        slot = len(members) * groups + at
                        first, final = w[0, r + 1], w[tiles - 1, r + 1]
                    edge = jnp.where(lane < LANES // 2, first, final)
                    moved = pltpu.roll(edge, (4 * slot + 2) % LANES, 1)
                    packed = jnp.where(lane // 4 == slot, moved, packed)
            pack[h * SUB : (h + 1) * SUB, :] = packed

    def edge_copy(dr, dc):
        at = (1 - dr) * 2 + (0 if dc > 0 else 1)
        size = 2 * SUB if dr == 0 else SUB
        return pltpu.make_async_remote_copy(
            src_ref=pack.at[pl.ds(0, size)], dst_ref=nb.at[at, pl.ds(0, size)],
            send_sem=col_send.at[at], recv_sem=col_recv.at[at],
            device_id=at_offset(dr, dc), device_id_type=MESH,
        )

    def row_copies(dr):
        src = 2 if dr < 0 else rows
        dst = rows + 2 if dr < 0 else 0
        at = 1 if dr < 0 else 0
        refs = [(
            w.at[pl.ds(0, tiles), 1 if dr < 0 else rows],
            w.at[pl.ds(0, tiles), rows + 1 if dr < 0 else 0],
        )]
        for t in range(tiles):
            refs.append((x.at[t, pl.ds(src, 2)], x.at[t, pl.ds(dst, 2)]))
        return [
            pltpu.make_async_remote_copy(
                src_ref=a, dst_ref=b, send_sem=row_send.at[at, k], recv_sem=row_recv.at[at, k],
                device_id=at_offset(dr, 0), device_id_type=MESH,
            )
            for k, (a, b) in enumerate(refs)
        ]

    with jax.named_scope("barrier"):
        pl.semaphore_wait(barrier, neighbours)
    with jax.named_scope("sends"):
        for dr, dc in around[:6]:
            @pl.when(cond(ups[dr], sides[dc]))
            def _(dr=dr, dc=dc):
                edge_copy(dr, dc).start()
        for dr in (-1, 1):
            @pl.when(ups[dr])
            def _(dr=dr):
                for copy in row_copies(dr):
                    copy.start()
        if rounds > 1:
            greet(reach.at[0])

    for dr in (-1, 1):
        @pl.when(jnp.logical_not(ups[dr]))
        def _(dr=dr):
            e = 0 if dr < 0 else rows + 2
            for t in range(tiles):
                x[t, e : e + 2] = jnp.zeros((2, n, LANES), f32)
                w[t, 0 if dr < 0 else rows + 1] = jnp.zeros((SUB, LANES), f32)
    for dr, dc in around[:6]:
        at = (1 + dr) * 2 + (1 if dc > 0 else 0)
        @pl.when(jnp.logical_not(cond(ups[dr], sides[dc])))
        def _(at=at):
            nb[at] = jnp.zeros((2 * SUB, LANES), f32)

    edge = tiles
    main = list(range(tiles))
    taken = (lane >= LANES - 2) | ((lane >= 64) & (lane < 66))

    def merge(at, h):
        part = pl.ds(h * SUB, SUB)
        return jnp.where(lane % 4 < 2, nb[at, part, :], pltpu.roll(nb[at + 1, part, :], 64, 1))

    def unpack(both, slot):
        return pltpu.roll(both, (-(4 * slot + 2)) % LANES, 1)

    def near(first, final):
        return jnp.where((lane >= 32) & (lane < 96), pltpu.roll(final, 64, 1), first)

    def shift_weights(r, ring):
        size = len(ring)
        taps = [w[t, r + 1] for t in ring]
        ahead = [pltpu.roll(v, LANES - 1, 1) for v in taps]
        behind = [pltpu.roll(v, 1, 1) for v in taps]
        left_taps = (sub == 0) | (sub == 3) | (sub == 5)
        right_taps = (sub == 2) | (sub == 4) | (sub == 7)
        for k, t in enumerate(ring):
            after, before = ahead[k], behind[k]
            if size > 1:
                after = jnp.where(lane == LANES - 1, ahead[(k + 1) % size], after)
                before = jnp.where(lane == 0, behind[k - 1], before)
            ws[t, r + 1, 0:SUB, :] = jnp.where(
                left_taps, after, jnp.where(right_taps, before, taps[k])
            )
            degree = jnp.sum(taps[k], axis=0, keepdims=True)
            ws[t, r + 1, SUB : 2 * SUB, :] = jnp.broadcast_to(degree, (SUB, LANES))

    def stencil(src, e, dst, d, r, ring):
        size = len(ring)
        parts = {}

        def write(k, g):
            center, low, high = parts[k, g]
            if size > 1:
                low = jnp.where(lane == 0, parts[(k - 1) % size, g][1], low)
                high = jnp.where(lane == LANES - 1, parts[(k + 1) % size, g][2], high)
            dst[ring[k], d, g * SUB : (g + 1) * SUB, :] = center + low + high

        for k, t in enumerate(ring):
            tap = [
                jnp.broadcast_to(ws[t, r + 1, pl.ds(q, 1), :], (SUB, LANES)) for q in range(SUB)
            ]
            degree = ws[t, r + 1, SUB : 2 * SUB, :]
            for g in range(groups):
                part = slice(g * SUB, (g + 1) * SUB)
                up, here, down = src[t, e - 1, part, :], src[t, e, part, :], src[t, e + 1, part, :]
                parts[k, g] = (
                    degree * here + tap[1] * up + tap[6] * down,
                    pltpu.roll(tap[0] * up + tap[3] * here + tap[5] * down, 1, 1),
                    pltpu.roll(tap[2] * up + tap[4] * here + tap[7] * down, LANES - 1, 1),
                )
                if k >= 2:
                    write(k - 1, g)
        for k in sorted({0, size - 1}):
            for g in range(groups):
                write(k, g)

    def gram(src, picks):
        pieces = []
        for d, with_main, with_edge in picks:
            if with_main:
                for t in main:
                    v = src[t, d]
                    if t == 0:
                        v = jnp.where(wide_lane >= 2, v, 0.0)
                    if t == tiles - 1:
                        v = jnp.where(wide_lane < LANES - 2, v, 0.0)
                    pieces.append(v)
            if with_edge:
                pieces.append(jnp.where(wide_edge, src[edge, d], 0.0))
        both = jnp.concatenate(split(jnp.concatenate(pieces, axis=1)), axis=0)
        return lax.dot_general(both, both, NT, preferred_element_type=f32)

    wide_lane = lax.broadcasted_iota(jnp.int32, (n, LANES), 1)
    wide_edge = (wide_lane < 2) | ((wide_lane >= 62) & (wide_lane < 64))

    with jax.named_scope("weights"):
        for r in range(rows):
            shift_weights(r, main)
    with jax.named_scope("y1in"):
        for r in range(1, rows - 1):
            stencil(x, r + 2, y1, r + 1, r, main)
    with jax.named_scope("y2in"):
        for r in range(2, rows - 2):
            stencil(y1, r + 1, y2, r, r, main)
    with jax.named_scope("nearedge"):
        for r in range(rows):
            for g in range(groups):
                part = slice(g * SUB, (g + 1) * SUB)
                x[edge, r + 2, part, :] = near(x[0, r + 2, part, :], x[tiles - 1, r + 2, part, :])
            w[edge, r + 1] = near(w[0, r + 1], w[tiles - 1, r + 1])
    with jax.named_scope("gramin"):
        total_1 = gram(y1, [(r + 1, True, False) for r in range(1, rows - 1)])
        total_2 = gram(y2, [(r, True, False) for r in range(2, rows - 2)])

    if rounds > 1:
        with jax.named_scope("round2"):
            pl.semaphore_wait(reach.at[0], neighbours)
            if rounds > 2:
                greet(reach.at[1])

    with jax.named_scope("recvcols"):
        for dc in (-1, 1):
            @pl.when(sides[dc])
            def _(dc=dc):
                edge_copy(0, -dc).wait_recv()
    with jax.named_scope("edges"):
        for h, members in enumerate(halves):
            both = merge(2, h)
            for at, r in enumerate(members):
                for g in range(groups):
                    part = slice(g * SUB, (g + 1) * SUB)
                    x[edge, r + 2, part, :] = jnp.where(
                        taken, unpack(both, at * groups + g), x[edge, r + 2, part, :]
                    )
                w[edge, r + 1] = jnp.where(
                    taken, unpack(both, len(members) * groups + at), w[edge, r + 1]
                )
        for r in range(rows):
            shift_weights(r, [edge])
        for r in range(1, rows - 1):
            stencil(x, r + 2, y1, r + 1, r, [edge])
        for r in range(2, rows - 2):
            stencil(y1, r + 1, y2, r, r, [edge])
        total_1 = total_1 + gram(y1, [(r + 1, False, True) for r in range(1, rows - 1)])
        total_2 = total_2 + gram(y2, [(r, False, True) for r in range(2, rows - 2)])

    def side(step, carry):
        total_1, total_2 = carry
        low = lax.rem(i + 1 + step, 2)
        for dr in (-1, 1):
            @pl.when(cond(low == (0 if dr < 0 else 1), ups[dr]))
            def _(dr=dr):
                for dc in (-1, 1):
                    @pl.when(sides[dc])
                    def _(dc=dc):
                        edge_copy(-dr, -dc).wait_recv()
                for copy in row_copies(-dr):
                    copy.wait_recv()
        both = merge(low * 4, 0)
        tap_both = jnp.where(
            low == 0, unpack(both, 4 * groups + 3), unpack(both, 4 * groups)
        )
        both = jnp.where(low == 0, pltpu.roll(both, LANES - 8 * groups, 1), both)
        for k in range(2):
            e = low * (rows + 2) + k
            for g in range(groups):
                part = slice(g * SUB, (g + 1) * SUB)
                x[edge, e, part, :] = jnp.where(
                    taken, unpack(both, k * groups + g),
                    near(x[0, e, part, :], x[tiles - 1, e, part, :]),
                )
        e = low * (rows + 1)
        w[edge, e] = jnp.where(taken, tap_both, near(w[0, e], w[tiles - 1, e]))
        for ring in (main, [edge]):
            shift_weights(e - 1, ring)
        for ring in (main, [edge]):
            for k in range(2):
                r = low * rows - 1 + k
                stencil(x, r + 2, y1, r + 1, r, ring)
        for ring in (main, [edge]):
            for k in range(2):
                r = low * (rows - 2) + k
                stencil(y1, r + 1, y2, r, r, ring)
        total_1 = total_1 + gram(y1, [(low * (rows - 1) + 1, True, True)])
        total_2 = total_2 + gram(y2, [(low * (rows - 2) + k, True, True) for k in range(2)])
        return total_1, total_2

    with jax.named_scope("sides"):
        total_1, total_2 = lax.fori_loop(0, 2, side, (total_1, total_2))

    scale = 1.0 / (rows * cols * R * C)

    def fold(total):
        half = total[0:n] + total[n : 2 * n]
        square = (half[:, 0:n] + half[:, n : 2 * n]) * scale
        return jnp.concatenate([square[g * SUB : (g + 1) * SUB] for g in range(groups)], axis=1)

    def gather_copies(stage, receiving):
        axes, count = stages[stage]
        me = {"row": i, "col": j, "both": j * R + i}[axes]
        copies = []
        for k in range(count - 1):
            peer = k + (k >= me).astype(jnp.int32)
            slot = peer if receiving else me
            target = {
                "row": {"row": peer, "col": j},
                "col": {"row": i, "col": peer},
                "both": {"row": lax.rem(peer, R), "col": lax.div(peer, R)},
            }[axes]
            copies.append(pltpu.make_async_remote_copy(
                src_ref=sent.at[stage], dst_ref=held.at[stage, slot],
                send_sem=gather_send.at[stage, k],
                recv_sem=gather_recv.at[stage, slot],
                device_id=target, device_id_type=MESH,
            ))
        return copies

    def spread(stage, value):
        axes, count = stages[stage]
        me = {"row": i, "col": j, "both": j * R + i}[axes]
        sent[stage] = value
        held[stage, me] = value
        for copy in gather_copies(stage, False):
            copy.start()

    def collect(stage):
        for copy in gather_copies(stage, True):
            copy.wait_recv()
        terms = [held[stage, at] for at in range(stages[stage][1])]
        while len(terms) > 1:
            terms = [sum(terms[k + 1 : k + 2], terms[k]) for k in range(0, len(terms), 2)]
        return terms[0]

    with jax.named_scope("fold"):
        value = jnp.concatenate([fold(total_1), fold(total_2)], axis=0)
    for k in range(2, rounds):
        with jax.named_scope("round3"):
            pl.semaphore_wait(reach.at[k - 1], neighbours)
            if k + 1 < rounds:
                greet(reach.at[k])
    with jax.named_scope("spread"):
        spread(0, value)

    def eliminate(square, step=4):
        blocks = []
        half = lane % 64
        for g in range(groups):
            mine_1, mine_2 = square[0:SUB], square[SUB : 2 * SUB]
            if g > 0:
                mine_1 = pltpu.roll(mine_1, LANES - g * n, 1)
            if g != 2:
                mine_2 = pltpu.roll(mine_2, (64 - g * n) % LANES, 1)
            eye = (half - n == sub + g * SUB).astype(f32)
            blocks.append(jnp.where(half < n, jnp.where(lane < 64, mine_1, mine_2), eye))

        def over_lanes(v, p):
            return jnp.where(
                lane < 64,
                jnp.broadcast_to(v[:, p : p + 1], (SUB, LANES)),
                jnp.broadcast_to(v[:, 64 + p : 64 + p + 1], (SUB, LANES)),
            )

        for p in range(0, n, step):
            home, base = p // SUB, p % SUB
            line = [
                jnp.broadcast_to(blocks[home][base + q : base + q + 1, :], (SUB, LANES))
                for q in range(step)
            ]
            column = {
                (s, g): over_lanes(blocks[g], p + s)
                for g in range(home, groups)
                for s in range(step)
            }
            corner = {
                (q, s): jnp.broadcast_to(column[s, home][base + q : base + q + 1, :], (SUB, LANES))
                for q in range(step)
                for s in range(q, step)
            }
            scaled = []
            for q in range(step):
                over = 1.0 / corner[q, q]
                scaled.append(line[q] * over)
                ratio = {s: corner[q, s] * over for s in range(q + 1, step)}
                for s in range(q + 1, step):
                    line[s] = line[s] - ratio[s] * line[q]
                    for t in range(s, step):
                        corner[s, t] = corner[s, t] - ratio[s] * corner[q, t]
                    for g in range(home, groups):
                        column[s, g] = column[s, g] - ratio[s] * column[q, g]
            for g in range(home, groups):
                if g == home and base + step == SUB:
                    continue
                update = column[0, g] * scaled[0]
                for q in range(1, step):
                    update = update + column[q, g] * scaled[q]
                if g == home:
                    update = jnp.where(sub >= base + step, update, 0.0)
                blocks[g] = blocks[g] - update
            for q in range(step):
                done = line[q] * (1.0 / jnp.sqrt(corner[q, q]))
                blocks[home] = jnp.where(sub == base + q, done, blocks[home])
        return jnp.concatenate(blocks, axis=0)

    for stage in range(1, len(stages)):
        spread(stage, collect(stage - 1))
    with jax.named_scope("patch"):
        for r in range(rows):
            edges = y2[edge, r]
            pieces = [y2[t, r] for t in main]
            pieces[0] = jnp.where(wide_lane < 2, edges, pieces[0])
            pieces[-1] = jnp.where(wide_lane >= LANES - 2, pltpu.roll(edges, 64, 1), pieces[-1])
            y2_out[r] = jnp.concatenate(split(jnp.concatenate(pieces, axis=1)), axis=0)
    with jax.named_scope("collect"):
        square = collect(len(stages) - 1)
    with jax.named_scope("eliminate"):
        tables[...] = eliminate(square)

    with jax.named_scope("drain"):
        for dr, dc in around[:6]:
            @pl.when(cond(ups[dr], sides[dc]))
            def _(dr=dr, dc=dc):
                edge_copy(dr, dc).wait_send()
        for dr in (-1, 1):
            @pl.when(ups[dr])
            def _(dr=dr):
                for copy in row_copies(dr):
                    copy.wait_send()
        for stage in range(len(stages)):
            for copy in gather_copies(stage, False):
                copy.wait_send()


def finish(n, rows, cols, y2, tables, out_ref, fac_ref, staged, fac, store_sem):
    groups = n // SUB
    tiles = cols // LANES
    inv_hi, inv_lo = split(tables[:, 3 * n : 4 * n])
    left = jnp.concatenate([inv_hi, inv_lo, inv_hi], axis=1)
    stores = []
    for t0 in range(0, tiles, 2):
        for r in range(rows):
            hi = y2[r, 0:n, t0 * LANES : (t0 + 2) * LANES]
            lo = y2[r, n : 2 * n, t0 * LANES : (t0 + 2) * LANES]
            right = jnp.concatenate([hi, hi, lo], axis=0)
            solved = jnp.dot(left, right, preferred_element_type=f32)
            for t in range(2):
                for g in range(groups):
                    staged[t0 + t, pl.ds(g * SUB * rows + r, SUB, stride=rows), :] = solved[
                        g * SUB : (g + 1) * SUB, t * LANES : (t + 1) * LANES
                    ]
        for t in range(t0, t0 + 2):
            stores.append(pltpu.make_async_copy(
                staged.at[t], out_ref.at[:, pl.ds(t * LANES, LANES)], store_sem.at[t]
            ))
            stores[-1].start()
    inverse_1 = tables[:, n : 2 * n]
    upper_2 = tables[:, 2 * n : 3 * n]
    row_at = lax.broadcasted_iota(jnp.int32, (n, n), 0)
    col_at = lax.broadcasted_iota(jnp.int32, (n, n), 1)
    upper_2 = jnp.where(col_at >= row_at, upper_2, 0.0)
    last = lax.dot_general(upper_2, inverse_1, NT, precision=HIGHEST, preferred_element_type=f32)
    fac[...] = jnp.where(col_at >= row_at, last, 0.0)
    stores.append(pltpu.make_async_copy(fac, fac_ref, store_sem.at[tiles]))
    stores[-1].start()
    for store in stores:
        store.wait()


def on_device(sketch, weights):
    n, rows, cols = sketch.shape
    R, C = lax.axis_size("row"), lax.axis_size("col")
    tiles = cols // LANES
    stages = (("both", R * C),) if R * C <= 16 else (("row", R), ("col", C))
    rounds = max(R, C) - 1
    peers = max(count for _, count in stages)
    dma = pltpu.SemaphoreType.DMA
    image, tables = pl.pallas_call(
        functools.partial(kernel, n, rows, cols, R, C, stages, rounds),
        out_shape=(
            pltpu.VMEM((rows, 2 * n, cols), bf16),
            pltpu.VMEM((n, LANES), f32),
        ),
        in_specs=[pl.BlockSpec(memory_space=pltpu.HBM)] * 2,
        out_specs=(
            pl.BlockSpec(memory_space=pltpu.VMEM),
            pl.BlockSpec(memory_space=pltpu.VMEM),
        ),
        scratch_shapes=[
            pltpu.VMEM((tiles, n * rows, LANES), f32),
            pltpu.VMEM((tiles, SUB * rows, LANES), f32),
            pltpu.VMEM((tiles + 1, rows + 4, n, LANES), f32),
            pltpu.VMEM((tiles + 1, rows + 2, SUB, LANES), f32),
            pltpu.VMEM((tiles + 1, rows + 2, 2 * SUB, LANES), f32),
            pltpu.VMEM((tiles + 1, rows + 2, n, LANES), f32),
            pltpu.VMEM((tiles + 1, rows, n, LANES), f32),
            pltpu.VMEM((2 * SUB, LANES), f32),
            pltpu.VMEM((6, 2 * SUB, LANES), f32),
            pltpu.VMEM((len(stages), peers, 2 * SUB, LANES), f32),
            pltpu.VMEM((len(stages), 2 * SUB, LANES), f32),
            dma((2, tiles)), dma((6,)), dma((6,)), dma((2, tiles + 1)), dma((2, tiles + 1)),
            dma((len(stages), peers)), dma((len(stages), peers)),
            pltpu.SemaphoreType.REGULAR((max(rounds - 1, 1),)),
        ],
        compiler_params=pltpu.CompilerParams(
            collective_id=0, has_side_effects=True, vmem_limit_bytes=16 * 1024 * 1024
        ),
    )(
        pltpu.with_memory_space_constraint(sketch.reshape(n * rows, cols), pltpu.HBM),
        pltpu.with_memory_space_constraint(weights.reshape(SUB * rows, cols), pltpu.HBM),
    )
    basis, factor = pl.pallas_call(
        functools.partial(finish, n, rows, cols),
        out_shape=(
            jax.ShapeDtypeStruct((n * rows, cols), f32),
            jax.ShapeDtypeStruct((n, n), f32),
        ),
        in_specs=[pl.BlockSpec(memory_space=pltpu.VMEM)] * 2,
        out_specs=(
            pl.BlockSpec(memory_space=pl.ANY),
            pl.BlockSpec(memory_space=pl.ANY),
        ),
        scratch_shapes=[
            pltpu.VMEM((tiles, n * rows, LANES), f32),
            pltpu.VMEM((n, n), f32),
            dma((tiles + 1,)),
        ],
        compiler_params=pltpu.CompilerParams(vmem_limit_bytes=16 * 1024 * 1024),
    )(image, tables)
    return basis.reshape(n, rows, cols), factor


def solution(mesh):
    return jax.shard_map(
        on_device,
        mesh=mesh,
        in_specs=(P(None, ("sec", "row"), "col"), P(None, ("sec", "row"), "col")),
        out_specs=(P(None, ("sec", "row"), "col"), P("sec", None)),
        check_vma=False,
    )
```

```python
import functools

import jax
import jax.numpy as jnp
from jax import lax
from jax.experimental import pallas as pl
from jax.experimental.pallas import tpu as pltpu
from jax.sharding import PartitionSpec as P

LANES = 128
SUB = 8
MESH = pl.DeviceIdType.MESH
NT = (((1,), (1,)), ((), ()))
HIGHEST = lax.Precision.HIGHEST
f32 = jnp.float32
bf16 = jnp.bfloat16


def split(x):
    hi = x.astype(bf16)
    lo = (x - hi.astype(f32)).astype(bf16)
    return hi, lo


def kernel(
    n, rows, cols, R, C, stages, rounds,
    sk_hbm, w_hbm, y2_out, tables,
    raw, wraw, x, w, ws, y1, y2, pack, nb, held, sent,
    load_sem, col_send, col_recv, row_send, row_recv, gather_send, gather_recv, reach,
):
    groups = n // SUB
    tiles = cols // LANES
    i = lax.axis_index("row")
    j = lax.axis_index("col")
    flip = 1 - lax.rem(i, 2)
    near_i = i + 2 * flip - 1
    far_i = i + 1 - 2 * flip
    has_far = (far_i >= 0) & (far_i < R)
    has_left, has_right = j > 0, j < C - 1

    kinds = ((i, None), (near_i, None), (far_i, has_far))
    SAME, NEAR, FAR = range(3)
    sides = {-1: has_left, 0: None, 1: has_right}
    beside = [(FAR, 0), (NEAR, 0)]
    around = [(kind, dc) for kind in (SAME, FAR, NEAR) for dc in (-1, 1)]

    def when(kind, dc):
        terms = [t for t in (kinds[kind][1], sides[dc]) if t is not None]
        if not terms:
            return lambda body: body()
        return pl.when(functools.reduce(jnp.logical_and, terms))

    def unless(kind, dc):
        terms = [t for t in (kinds[kind][1], sides[dc]) if t is not None]
        if not terms:
            return lambda body: None
        return pl.when(jnp.logical_not(functools.reduce(jnp.logical_and, terms)))

    def at_offset(kind, dc):
        return {"row": kinds[kind][0], "col": j + dc}

    def greet(sem):
        for kind, dc in beside + around:
            @when(kind, dc)
            def _(kind=kind, dc=dc):
                pl.semaphore_signal(sem, inc=1, device_id=at_offset(kind, dc), device_id_type=MESH)

    height = 2 + has_far.astype(jnp.int32)
    breadth = 1 + has_left.astype(jnp.int32) + has_right.astype(jnp.int32)
    neighbours = height * breadth - 1

    barrier = pltpu.get_barrier_semaphore()
    greet(barrier)

    loads = []
    for t in range(tiles):
        across = pl.ds(t * LANES, LANES)
        loads.append(pltpu.make_async_copy(sk_hbm.at[:, across], raw.at[t], load_sem.at[0, t]))
        loads.append(pltpu.make_async_copy(w_hbm.at[:, across], wraw.at[t], load_sem.at[1, t]))
    for load in loads:
        load.start()

    lane = lax.broadcasted_iota(jnp.int32, (SUB, LANES), 1)
    sub = lax.broadcasted_iota(jnp.int32, (SUB, LANES), 0)

    with jax.named_scope("load"):
        for load in loads:
            load.wait()
    def mirror(v):
        return jnp.where(
            sub < 3, pltpu.roll(v, 3, 0), jnp.where(sub < 5, v, pltpu.roll(v, 5, 0))
        )

    def original(r):
        return r + flip * (rows - 1 - 2 * r)

    def relayout(members):
        for r in members:
            r0 = original(r)
            for t in range(tiles):
                for g in range(groups):
                    x[t, r + 2, g * SUB : (g + 1) * SUB, :] = raw[
                        t, pl.ds(g * SUB * rows + r0, SUB, stride=rows), :
                    ]
                v = wraw[t, pl.ds(r0, SUB, stride=rows), :]
                w[t, r + 1] = jnp.where(flip == 1, mirror(v), v)

    outer = [0, 1, rows - 2, rows - 1]
    inner = list(range(2, rows - 2))
    halves = (outer, inner)

    def edge_copy(kind, dc):
        at = 2 * kind + (0 if dc > 0 else 1)
        size = 2 * SUB if kind == SAME else SUB
        return pltpu.make_async_remote_copy(
            src_ref=pack.at[pl.ds(0, size)], dst_ref=nb.at[at, pl.ds(0, size)],
            send_sem=col_send.at[at], recv_sem=col_recv.at[at],
            device_id=at_offset(kind, dc), device_id_type=MESH,
        )

    def row_copies(kind, only=None):
        at = 0 if kind == NEAR else 1
        refs = [(
            w.at[pl.ds(0, tiles), 1 if kind == NEAR else rows],
            w.at[pl.ds(0, tiles), 0 if kind == NEAR else rows + 1],
        )]
        src, dst = (2, 0) if kind == NEAR else (rows, rows + 2)
        for t in range(tiles):
            refs.append((x.at[t, pl.ds(src, 2)], x.at[t, pl.ds(dst, 2)]))
        return [
            pltpu.make_async_remote_copy(
                src_ref=a, dst_ref=b, send_sem=row_send.at[at, k], recv_sem=row_recv.at[at, k],
                device_id=at_offset(kind, 0), device_id_type=MESH,
            )
            for k, (a, b) in enumerate(refs)
            if only is None or k in only
        ]

    with jax.named_scope("relayout"):
        relayout(outer)
    with jax.named_scope("barrier"):
        pl.semaphore_wait(barrier, neighbours)
    with jax.named_scope("rowsends"):
        for kind in (FAR, NEAR):
            @when(kind, 0)
            def _(kind=kind):
                for copy in row_copies(kind):
                    copy.start()
        if rounds > 1:
            greet(reach.at[0])
    with jax.named_scope("relayout2"):
        relayout(inner)
    with jax.named_scope("pack"):
        for h, members in enumerate(halves):
            packed = jnp.zeros((SUB, LANES), f32)
            for at, r in enumerate(members):
                for g in range(groups + 1):
                    if g < groups:
                        slot = at * groups + g
                        first = x[0, r + 2, g * SUB : (g + 1) * SUB, :]
                        final = x[tiles - 1, r + 2, g * SUB : (g + 1) * SUB, :]
                    else:
                        slot = len(members) * groups + at
                        first, final = w[0, r + 1], w[tiles - 1, r + 1]
                    edge = jnp.where(lane < LANES // 2, first, final)
                    moved = pltpu.roll(edge, (4 * slot + 2) % LANES, 1)
                    packed = jnp.where(lane // 4 == slot, moved, packed)
            pack[h * SUB : (h + 1) * SUB, :] = packed
    with jax.named_scope("sends"):
        for kind, dc in around:
            @when(kind, dc)
            def _(kind=kind, dc=dc):
                edge_copy(kind, dc).start()

    @unless(FAR, 0)
    def _():
        for t in range(tiles):
            x[t, rows + 2 : rows + 4] = jnp.zeros((2, n, LANES), f32)
            w[t, rows + 1] = jnp.zeros((SUB, LANES), f32)

    for kind, dc in around:
        @unless(kind, dc)
        def _(kind=kind, dc=dc):
            nb[2 * kind + (1 if dc > 0 else 0)] = jnp.zeros((2 * SUB, LANES), f32)

    edge = tiles
    main = list(range(tiles))
    taken = (lane >= LANES - 2) | ((lane >= 64) & (lane < 66))

    def merge(kind, h):
        at = 2 * kind
        part = pl.ds(h * SUB, SUB)
        return jnp.where(lane % 4 < 2, nb[at, part, :], pltpu.roll(nb[at + 1, part, :], 64, 1))

    def unpack(both, slot):
        return pltpu.roll(both, (-(4 * slot + 2)) % LANES, 1)

    def near(first, final):
        return jnp.where((lane >= 32) & (lane < 96), pltpu.roll(final, 64, 1), first)

    def shift_weights(r, ring):
        size = len(ring)
        taps = [w[t, r + 1] for t in ring]
        ahead = [pltpu.roll(v, LANES - 1, 1) for v in taps]
        behind = [pltpu.roll(v, 1, 1) for v in taps]
        left_taps = (sub == 0) | (sub == 3) | (sub == 5)
        right_taps = (sub == 2) | (sub == 4) | (sub == 7)
        for k, t in enumerate(ring):
            after, before = ahead[k], behind[k]
            if k + 1 < size:
                after = jnp.where(lane == LANES - 1, ahead[k + 1], after)
            if k > 0:
                before = jnp.where(lane == 0, behind[k - 1], before)
            ws[t, r + 1, 0:SUB, :] = jnp.where(
                left_taps, after, jnp.where(right_taps, before, taps[k])
            )
            degree = jnp.sum(taps[k], axis=0, keepdims=True)
            ws[t, r + 1, SUB : 2 * SUB, :] = jnp.broadcast_to(degree, (SUB, LANES))

    def stencil(src, dst, rows_at, ring):
        size = len(ring)
        parts = {}

        def begin(k):
            t = ring[k]
            for at, (near_by, d, r) in enumerate(rows_at):
                tap = [
                    jnp.broadcast_to(ws[t, r + 1, pl.ds(q, 1), :], (SUB, LANES))
                    for q in range(SUB)
                ]
                degree = ws[t, r + 1, SUB : 2 * SUB, :]
                for g in range(groups):
                    part = slice(g * SUB, (g + 1) * SUB)
                    up, here, down = (src[t, e, part, :] for e in near_by)
                    parts[k, at, g] = (
                        degree * here + tap[1] * up + tap[6] * down,
                        pltpu.roll(tap[0] * up + tap[3] * here + tap[5] * down, 1, 1),
                        pltpu.roll(tap[2] * up + tap[4] * here + tap[7] * down, LANES - 1, 1),
                    )

        def end(k):
            for at, (_, d, r) in enumerate(rows_at):
                for g in range(groups):
                    center, low, high = parts[k, at, g]
                    if k > 0:
                        low = jnp.where(lane == 0, parts[k - 1, at, g][1], low)
                    if k + 1 < size:
                        high = jnp.where(lane == LANES - 1, parts[k + 1, at, g][2], high)
                    dst[ring[k], d, g * SUB : (g + 1) * SUB, :] = center + low + high

        return begin, end

    def whole_rows(src, dst, rows_at, ring):
        for row_at in rows_at:
            begin, end = stencil(src, dst, [row_at], ring)
            for k in range(len(ring)):
                begin(k)
                if k > 0:
                    end(k - 1)
            end(len(ring) - 1)

    def x_row(r):
        return {-1: 0, -2: 1, rows: rows + 3, rows + 1: rows + 2}.get(r, r + 2)

    def first_image(members):
        return [((x_row(r - 1), x_row(r), x_row(r + 1)), r + 1, r) for r in members]

    def second_image(members):
        return [((r, r + 1, r + 2), r, r) for r in members]

    def gram(src, picks):
        pieces = []
        for d, with_main, with_edge in picks:
            if with_main:
                for t in main:
                    v = src[t, d]
                    if t == 0:
                        v = jnp.where(wide_lane >= 2, v, 0.0)
                    if t == tiles - 1:
                        v = jnp.where(wide_lane < LANES - 2, v, 0.0)
                    pieces.append(v)
            if with_edge:
                pieces.append(jnp.where(wide_edge, src[edge, d], 0.0))
        both = jnp.concatenate(split(jnp.concatenate(pieces, axis=1)), axis=0)
        return lax.dot_general(both, both, NT, preferred_element_type=f32)

    wide_lane = lax.broadcasted_iota(jnp.int32, (n, LANES), 1)
    wide_edge = (wide_lane < 2) | ((wide_lane >= 62) & (wide_lane < 64))

    with jax.named_scope("weights"):
        for r in range(rows):
            shift_weights(r, main)
    with jax.named_scope("y1in"):
        whole_rows(x, y1, first_image(range(1, rows - 1)), main)
    with jax.named_scope("y2in"):
        whole_rows(y1, y2, second_image(range(2, rows - 2)), main)
    with jax.named_scope("gramin"):
        total_1 = gram(y1, [(r + 1, True, False) for r in range(1, rows - 1)])
        total_2 = gram(y2, [(r, True, False) for r in range(2, rows - 2)])

    if rounds > 1:
        with jax.named_scope("round2"):
            pl.semaphore_wait(reach.at[0], neighbours)
            if rounds > 2:
                greet(reach.at[1])

    def build_edge(kind, members, part_of):
        half, size = part_of
        both = merge(kind, half)
        for r, at in members:
            e = x_row(r)
            for g in range(groups):
                part = slice(g * SUB, (g + 1) * SUB)
                x[edge, e, part, :] = jnp.where(
                    taken, unpack(both, at * groups + g),
                    near(x[0, e, part, :], x[tiles - 1, e, part, :]),
                )
        for r, at in members:
            if -1 <= r <= rows:
                v = unpack(both, size * groups + at)
                if kind != SAME:
                    v = mirror(v)
                w[edge, r + 1] = jnp.where(taken, v, near(w[0, r + 1], w[tiles - 1, r + 1]))

    with jax.named_scope("recvnear"):
        for copy in row_copies(NEAR):
            copy.wait_recv()
    with jax.named_scope("near"):
        for t in main:
            w[t, 0] = mirror(w[t, 0])
        shift_weights(-1, main)
        whole_rows(x, y1, first_image((-1, 0)), main)
        whole_rows(y1, y2, second_image((0, 1)), main)
        total_1 = total_1 + gram(y1, [(1, True, False)])
        total_2 = total_2 + gram(y2, [(r, True, False) for r in (0, 1)])

    with jax.named_scope("recvcols"):
        for kind in (SAME, NEAR):
            for dc in (-1, 1):
                @when(kind, dc)
                def _(kind=kind, dc=dc):
                    edge_copy(kind, -dc).wait_recv()
    with jax.named_scope("edges"):
        for h, members in enumerate(halves):
            build_edge(SAME, [(r, at) for at, r in enumerate(members)], (h, len(members)))
        build_edge(NEAR, [(-1, 0), (-2, 1)], (0, len(outer)))
        for r in range(-1, rows):
            shift_weights(r, [edge])
        whole_rows(x, y1, first_image(range(-1, rows - 1)), [edge])
        whole_rows(y1, y2, second_image(range(rows - 2)), [edge])
        total_1 = total_1 + gram(y1, [(r + 1, False, True) for r in range(rows - 1)])
        total_2 = total_2 + gram(y2, [(r, False, True) for r in range(rows - 2)])

    with jax.named_scope("recvfar1"):
        @when(FAR, 0)
        def _():
            for dc in (-1, 1):
                @when(SAME, dc)
                def _(dc=dc):
                    edge_copy(FAR, -dc).wait_recv()
            row_copies(FAR, (0,))[0].wait_recv()
    with jax.named_scope("far1"):
        for t in main:
            w[t, rows + 1] = mirror(w[t, rows + 1])
        both = merge(FAR, 0)
        v = mirror(unpack(both, len(outer) * groups + 3))
        w[edge, rows + 1] = jnp.where(taken, v, near(w[0, rows + 1], w[tiles - 1, rows + 1]))
        for ring in (main, [edge]):
            shift_weights(rows, ring)
    with jax.named_scope("recvfar2"):
        @when(FAR, 0)
        def _():
            for copy in row_copies(FAR, range(1, tiles + 1)):
                copy.wait_recv()
    with jax.named_scope("far2"):
        for r, at in ((rows, 3), (rows + 1, 2)):
            e = x_row(r)
            for g in range(groups):
                part = slice(g * SUB, (g + 1) * SUB)
                x[edge, e, part, :] = jnp.where(
                    taken, unpack(both, at * groups + g),
                    near(x[0, e, part, :], x[tiles - 1, e, part, :]),
                )
        for ring in (main, [edge]):
            whole_rows(x, y1, first_image((rows - 1, rows)), ring)
        for ring in (main, [edge]):
            whole_rows(y1, y2, second_image((rows - 2, rows - 1)), ring)
        total_1 = total_1 + gram(y1, [(rows, True, True)])
        total_2 = total_2 + gram(y2, [(r, True, True) for r in (rows - 2, rows - 1)])

    scale = 1.0 / (rows * cols * R * C)

    def fold(total):
        half = total[0:n] + total[n : 2 * n]
        square = (half[:, 0:n] + half[:, n : 2 * n]) * scale
        return jnp.concatenate([square[g * SUB : (g + 1) * SUB] for g in range(groups)], axis=1)

    def gather_copies(stage, receiving):
        axes, count = stages[stage]
        me = {"row": i, "col": j, "both": j * R + i}[axes]
        copies = []
        for k in range(count - 1):
            peer = k + (k >= me).astype(jnp.int32)
            slot = peer if receiving else me
            target = {
                "row": {"row": peer, "col": j},
                "col": {"row": i, "col": peer},
                "both": {"row": lax.rem(peer, R), "col": lax.div(peer, R)},
            }[axes]
            copies.append(pltpu.make_async_remote_copy(
                src_ref=sent.at[stage], dst_ref=held.at[stage, slot],
                send_sem=gather_send.at[stage, k],
                recv_sem=gather_recv.at[stage, slot],
                device_id=target, device_id_type=MESH,
            ))
        return copies

    def spread(stage, value, diagonal):
        axes, count = stages[stage]
        me = {"row": i, "col": j, "both": j * R + i}[axes]
        for ref in (sent.at[stage], held.at[stage, me]):
            ref[0:SUB, :] = value
            ref[SUB : SUB + 1, :] = diagonal
        for copy in gather_copies(stage, False):
            copy.start()

    def collect(stage):
        for copy in gather_copies(stage, True):
            copy.wait_recv()
        totals = []
        for part in (slice(0, SUB), slice(SUB, SUB + 1)):
            terms = [held[stage, at, part, :] for at in range(stages[stage][1])]
            while len(terms) > 1:
                terms = [sum(terms[k + 1 : k + 2], terms[k]) for k in range(0, len(terms), 2)]
            totals.append(terms[0])
        return totals

    with jax.named_scope("fold"):
        across, down = lane % n, sub + SUB * (lane // n)
        folded = fold(total_2)
        value = jnp.where(across >= down, fold(total_1), folded)
        diagonal = jnp.sum(jnp.where(across == down, folded, 0.0), axis=0, keepdims=True)
    for k in range(2, rounds):
        with jax.named_scope("round3"):
            pl.semaphore_wait(reach.at[k - 1], neighbours)
            if k + 1 < rounds:
                greet(reach.at[k])
    with jax.named_scope("spread"):
        spread(0, value, diagonal)

    def eliminate(square, diagonal, step=SUB):
        blocks = []
        half = lane % 64
        stacked = jnp.concatenate(
            [square] + [pltpu.roll(square, LANES - g * n, 1) for g in range(1, groups)], axis=0
        )
        turned = stacked.T[0:n]
        diagonal = jnp.broadcast_to(diagonal, (SUB, LANES))
        for g in range(groups):
            part = slice(g * SUB, (g + 1) * SUB)
            row = sub + g * SUB
            mirror = jnp.concatenate([turned[part]] * (LANES // n), axis=1)
            whole = jnp.concatenate([stacked[part, 0:n]] * (LANES // n), axis=1)
            shifted = pltpu.roll(diagonal, (64 - g * n) % LANES, 1)
            first = jnp.where(lane >= row, whole, mirror)
            second = jnp.where(half < row, whole, jnp.where(half == row, shifted, mirror))
            eye = (half - n == row).astype(f32)
            blocks.append(jnp.where(half < n, jnp.where(lane < 64, first, second), eye))

        def over_lanes(v, p):
            return jnp.where(
                lane < 64,
                jnp.broadcast_to(v[:, p : p + 1], (SUB, LANES)),
                jnp.broadcast_to(v[:, 64 + p : 64 + p + 1], (SUB, LANES)),
            )

        solved = [jnp.zeros((SUB, LANES), f32)] * groups
        for p in range(0, n, step):
            home, base = p // SUB, p % SUB
            line = [
                jnp.broadcast_to(blocks[home][base + q : base + q + 1, :], (SUB, LANES))
                for q in range(step)
            ]
            column = {
                (s, g): over_lanes(blocks[g], p + s)
                for g in range(home, groups)
                for s in range(step)
            }
            corner = {
                (q, s): jnp.broadcast_to(column[s, home][base + q : base + q + 1, :], (SUB, LANES))
                for q in range(step)
                for s in range(q, step)
            }
            scaled = []
            for q in range(step):
                over = 1.0 / corner[q, q]
                scaled.append(line[q] * over)
                ratio = {s: corner[q, s] * over for s in range(q + 1, step)}
                for s in range(q + 1, step):
                    line[s] = line[s] - ratio[s] * line[q]
                    for t in range(s, step):
                        corner[s, t] = corner[s, t] - ratio[s] * corner[q, t]
                    for g in range(home + (base + step == SUB), groups):
                        column[s, g] = column[s, g] - ratio[s] * column[q, g]
            for g in range(home + (base + step == SUB), groups):
                update = column[0, g] * scaled[0]
                for q in range(1, step):
                    update = update + column[q, g] * scaled[q]
                blocks[g] = blocks[g] - update
            for q in range(step):
                done = line[q] * lax.rsqrt(corner[q, q])
                solved[home] = jnp.where(sub == base + q, done, solved[home])
        return jnp.concatenate(solved, axis=0)

    for stage in range(1, len(stages)):
        spread(stage, *collect(stage - 1))
    with jax.named_scope("patch"):
        for r in range(rows):
            edges = y2[edge, r]
            pieces = [y2[t, r] for t in main]
            pieces[0] = jnp.where(wide_lane < 2, edges, pieces[0])
            pieces[-1] = jnp.where(wide_lane >= LANES - 2, pltpu.roll(edges, 64, 1), pieces[-1])
            y2_out[original(r)] = jnp.concatenate(split(jnp.concatenate(pieces, axis=1)), axis=0)
    with jax.named_scope("collect"):
        square, diagonal = collect(len(stages) - 1)
    with jax.named_scope("eliminate"):
        tables[...] = eliminate(square, diagonal)

    with jax.named_scope("drain"):
        for kind, dc in around:
            @when(kind, dc)
            def _(kind=kind, dc=dc):
                edge_copy(kind, dc).wait_send()
        for kind in (NEAR, FAR):
            @when(kind, 0)
            def _(kind=kind):
                for copy in row_copies(kind):
                    copy.wait_send()
        for stage in range(len(stages)):
            for copy in gather_copies(stage, False):
                copy.wait_send()


def finish(n, rows, cols, y2, tables, out_ref, fac_ref, staged, fac, store_sem):
    groups = n // SUB
    tiles = cols // LANES
    inv_hi, inv_lo = split(tables[:, 3 * n : 4 * n])
    left = jnp.concatenate([inv_hi, inv_lo, inv_hi], axis=1)
    stores = []
    for t0 in range(0, tiles, 2):
        for r in range(rows):
            hi = y2[r, 0:n, t0 * LANES : (t0 + 2) * LANES]
            lo = y2[r, n : 2 * n, t0 * LANES : (t0 + 2) * LANES]
            right = jnp.concatenate([hi, hi, lo], axis=0)
            solved = jnp.dot(left, right, preferred_element_type=f32)
            for t in range(2):
                for g in range(groups):
                    staged[t0 + t, pl.ds(g * SUB * rows + r, SUB, stride=rows), :] = solved[
                        g * SUB : (g + 1) * SUB, t * LANES : (t + 1) * LANES
                    ]
        for t in range(t0, t0 + 2):
            stores.append(pltpu.make_async_copy(
                staged.at[t], out_ref.at[:, pl.ds(t * LANES, LANES)], store_sem.at[t]
            ))
            stores[-1].start()
    inverse_1 = tables[:, n : 2 * n]
    upper_2 = tables[:, 2 * n : 3 * n]
    row_at = lax.broadcasted_iota(jnp.int32, (n, n), 0)
    col_at = lax.broadcasted_iota(jnp.int32, (n, n), 1)
    upper_2 = jnp.where(col_at >= row_at, upper_2, 0.0)
    last = lax.dot_general(upper_2, inverse_1, NT, precision=HIGHEST, preferred_element_type=f32)
    fac[...] = jnp.where(col_at >= row_at, last, 0.0)
    stores.append(pltpu.make_async_copy(fac, fac_ref, store_sem.at[tiles]))
    stores[-1].start()
    for store in stores:
        store.wait()


def on_device(sketch, weights):
    n, rows, cols = sketch.shape
    R, C = lax.axis_size("row"), lax.axis_size("col")
    tiles = cols // LANES
    stages = (("both", R * C),) if R * C <= 16 else (("row", R), ("col", C))
    rounds = max(R, C) - 1
    peers = max(count for _, count in stages)
    dma = pltpu.SemaphoreType.DMA
    image, tables = pl.pallas_call(
        functools.partial(kernel, n, rows, cols, R, C, stages, rounds),
        out_shape=(
            pltpu.VMEM((rows, 2 * n, cols), bf16),
            pltpu.VMEM((n, LANES), f32),
        ),
        in_specs=[pl.BlockSpec(memory_space=pltpu.HBM)] * 2,
        out_specs=(
            pl.BlockSpec(memory_space=pltpu.VMEM),
            pl.BlockSpec(memory_space=pltpu.VMEM),
        ),
        scratch_shapes=[
            pltpu.VMEM((tiles, n * rows, LANES), f32),
            pltpu.VMEM((tiles, SUB * rows, LANES), f32),
            pltpu.VMEM((tiles + 1, rows + 4, n, LANES), f32),
            pltpu.VMEM((tiles + 1, rows + 2, SUB, LANES), f32),
            pltpu.VMEM((tiles + 1, rows + 2, 2 * SUB, LANES), f32),
            pltpu.VMEM((tiles + 1, rows + 2, n, LANES), f32),
            pltpu.VMEM((tiles + 1, rows, n, LANES), f32),
            pltpu.VMEM((2 * SUB, LANES), f32),
            pltpu.VMEM((6, 2 * SUB, LANES), f32),
            pltpu.VMEM((len(stages), peers, SUB + 1, LANES), f32),
            pltpu.VMEM((len(stages), SUB + 1, LANES), f32),
            dma((2, tiles)), dma((6,)), dma((6,)), dma((2, tiles + 1)), dma((2, tiles + 1)),
            dma((len(stages), peers)), dma((len(stages), peers)),
            pltpu.SemaphoreType.REGULAR((max(rounds - 1, 1),)),
        ],
        compiler_params=pltpu.CompilerParams(
            collective_id=0, has_side_effects=True, vmem_limit_bytes=16 * 1024 * 1024
        ),
    )(
        pltpu.with_memory_space_constraint(sketch.reshape(n * rows, cols), pltpu.HBM),
        pltpu.with_memory_space_constraint(weights.reshape(SUB * rows, cols), pltpu.HBM),
    )
    basis, factor = pl.pallas_call(
        functools.partial(finish, n, rows, cols),
        out_shape=(
            jax.ShapeDtypeStruct((n * rows, cols), f32),
            jax.ShapeDtypeStruct((n, n), f32),
        ),
        in_specs=[pl.BlockSpec(memory_space=pltpu.VMEM)] * 2,
        out_specs=(
            pl.BlockSpec(memory_space=pl.ANY),
            pl.BlockSpec(memory_space=pl.ANY),
        ),
        scratch_shapes=[
            pltpu.VMEM((tiles, n * rows, LANES), f32),
            pltpu.VMEM((n, n), f32),
            dma((tiles + 1,)),
        ],
        compiler_params=pltpu.CompilerParams(vmem_limit_bytes=16 * 1024 * 1024),
    )(image, tables)
    return basis.reshape(n, rows, cols), factor


def solution(mesh):
    return jax.shard_map(
        on_device,
        mesh=mesh,
        in_specs=(P(None, ("sec", "row"), "col"), P(None, ("sec", "row"), "col")),
        out_specs=(P(None, ("sec", "row"), "col"), P("sec", None)),
        check_vma=False,
    )
```

```python
import functools

import jax
import jax.numpy as jnp
from jax import lax
from jax.experimental import pallas as pl
from jax.experimental.pallas import tpu as pltpu
from jax.sharding import PartitionSpec as P

LANES = 128
SUB = 8
MESH = pl.DeviceIdType.MESH
NT = (((1,), (1,)), ((), ()))
HIGHEST = lax.Precision.HIGHEST
f32 = jnp.float32
bf16 = jnp.bfloat16


def split(x):
    hi = x.astype(bf16)
    lo = (x - hi.astype(f32)).astype(bf16)
    return hi, lo


def kernel(
    n, rows, cols, R, C, stages, rounds,
    sk_hbm, w_hbm, y2_out, tables,
    raw, wraw, x, w, ws, y1, y2, pack, nb, held, sent,
    load_sem, col_send, col_recv, row_send, row_recv, gather_send, gather_recv, reach,
):
    groups = n // SUB
    tiles = cols // LANES
    i = lax.axis_index("row")
    j = lax.axis_index("col")
    flip = 1 - lax.rem(i, 2)
    near_i = i + 2 * flip - 1
    far_i = i + 1 - 2 * flip
    has_far = (far_i >= 0) & (far_i < R)
    has_left, has_right = j > 0, j < C - 1

    kinds = ((i, None), (near_i, None), (far_i, has_far))
    SAME, NEAR, FAR = range(3)
    sides = {-1: has_left, 0: None, 1: has_right}
    beside = [(FAR, 0), (NEAR, 0)]
    around = [(kind, dc) for kind in (SAME, FAR, NEAR) for dc in (-1, 1)]

    def when(kind, dc):
        terms = [t for t in (kinds[kind][1], sides[dc]) if t is not None]
        if not terms:
            return lambda body: body()
        return pl.when(functools.reduce(jnp.logical_and, terms))

    def unless(kind, dc):
        terms = [t for t in (kinds[kind][1], sides[dc]) if t is not None]
        if not terms:
            return lambda body: None
        return pl.when(jnp.logical_not(functools.reduce(jnp.logical_and, terms)))

    def at_offset(kind, dc):
        return {"row": kinds[kind][0], "col": j + dc}

    def greet(sem):
        for kind, dc in beside + around:
            @when(kind, dc)
            def _(kind=kind, dc=dc):
                pl.semaphore_signal(sem, inc=1, device_id=at_offset(kind, dc), device_id_type=MESH)

    height = 2 + has_far.astype(jnp.int32)
    breadth = 1 + has_left.astype(jnp.int32) + has_right.astype(jnp.int32)
    neighbours = height * breadth - 1

    barrier = pltpu.get_barrier_semaphore()
    greet(barrier)

    loads = []
    for t in range(tiles):
        across = pl.ds(t * LANES, LANES)
        loads.append(pltpu.make_async_copy(sk_hbm.at[:, across], raw.at[t], load_sem.at[0, t]))
        loads.append(pltpu.make_async_copy(w_hbm.at[:, across], wraw.at[t], load_sem.at[1, t]))
    for load in loads:
        load.start()

    lane = lax.broadcasted_iota(jnp.int32, (SUB, LANES), 1)
    sub = lax.broadcasted_iota(jnp.int32, (SUB, LANES), 0)

    with jax.named_scope("load"):
        for load in loads:
            load.wait()
    def mirror(v):
        return jnp.where(
            sub < 3, pltpu.roll(v, 3, 0), jnp.where(sub < 5, v, pltpu.roll(v, 5, 0))
        )

    def original(r):
        return r + flip * (rows - 1 - 2 * r)

    def relayout(members):
        for r in members:
            r0 = original(r)
            for t in range(tiles):
                for g in range(groups):
                    x[t, r + 2, g * SUB : (g + 1) * SUB, :] = raw[
                        t, pl.ds(g * SUB * rows + r0, SUB, stride=rows), :
                    ]
                v = wraw[t, pl.ds(r0, SUB, stride=rows), :]
                w[t, r + 1] = jnp.where(flip == 1, mirror(v), v)

    outer = [0, 1, rows - 2, rows - 1]
    inner = list(range(2, rows - 2))
    halves = (outer, inner)

    def edge_copy(kind, dc):
        at = 2 * kind + (0 if dc > 0 else 1)
        size = 2 * SUB if kind == SAME else SUB
        return pltpu.make_async_remote_copy(
            src_ref=pack.at[pl.ds(0, size)], dst_ref=nb.at[at, pl.ds(0, size)],
            send_sem=col_send.at[at], recv_sem=col_recv.at[at],
            device_id=at_offset(kind, dc), device_id_type=MESH,
        )

    def row_copies(kind, only=None):
        at = 0 if kind == NEAR else 1
        refs = [(
            w.at[pl.ds(0, tiles), 1 if kind == NEAR else rows],
            w.at[pl.ds(0, tiles), 0 if kind == NEAR else rows + 1],
        )]
        src, dst = (2, 0) if kind == NEAR else (rows, rows + 2)
        for t in range(tiles):
            refs.append((x.at[t, pl.ds(src, 2)], x.at[t, pl.ds(dst, 2)]))
        return [
            pltpu.make_async_remote_copy(
                src_ref=a, dst_ref=b, send_sem=row_send.at[at, k], recv_sem=row_recv.at[at, k],
                device_id=at_offset(kind, 0), device_id_type=MESH,
            )
            for k, (a, b) in enumerate(refs)
            if only is None or k in only
        ]

    with jax.named_scope("relayout"):
        relayout(range(rows))
    with jax.named_scope("pack"):
        for h, members in enumerate(halves):
            packed = jnp.zeros((SUB, LANES), f32)
            for at, r in enumerate(members):
                for g in range(groups + 1):
                    if g < groups:
                        slot = at * groups + g
                        first = x[0, r + 2, g * SUB : (g + 1) * SUB, :]
                        final = x[tiles - 1, r + 2, g * SUB : (g + 1) * SUB, :]
                    else:
                        slot = len(members) * groups + at
                        first, final = w[0, r + 1], w[tiles - 1, r + 1]
                    edge = jnp.where(lane < LANES // 2, first, final)
                    moved = pltpu.roll(edge, (4 * slot + 2) % LANES, 1)
                    packed = jnp.where(lane // 4 == slot, moved, packed)
            pack[h * SUB : (h + 1) * SUB, :] = packed
    with jax.named_scope("barrier"):
        pl.semaphore_wait(barrier, neighbours)
    with jax.named_scope("sends"):
        for kind, dc in around:
            @when(kind, dc)
            def _(kind=kind, dc=dc):
                edge_copy(kind, dc).start()
    with jax.named_scope("rowsends"):
        for kind in (FAR, NEAR):
            @when(kind, 0)
            def _(kind=kind):
                for copy in row_copies(kind):
                    copy.start()
        if rounds > 1:
            greet(reach.at[0])

    @unless(FAR, 0)
    def _():
        for t in range(tiles):
            x[t, rows + 2 : rows + 4] = jnp.zeros((2, n, LANES), f32)
            w[t, rows + 1] = jnp.zeros((SUB, LANES), f32)

    for kind, dc in around:
        @unless(kind, dc)
        def _(kind=kind, dc=dc):
            nb[2 * kind + (1 if dc > 0 else 0)] = jnp.zeros((2 * SUB, LANES), f32)

    edge = tiles
    main = list(range(tiles))
    taken = (lane >= LANES - 2) | ((lane >= 64) & (lane < 66))

    def merge(kind, h):
        at = 2 * kind
        part = pl.ds(h * SUB, SUB)
        return jnp.where(lane % 4 < 2, nb[at, part, :], pltpu.roll(nb[at + 1, part, :], 64, 1))

    def unpack(both, slot):
        return pltpu.roll(both, (-(4 * slot + 2)) % LANES, 1)

    def near(first, final):
        return jnp.where((lane >= 32) & (lane < 96), pltpu.roll(final, 64, 1), first)

    def shift_weights(r, ring):
        size = len(ring)
        taps = [w[t, r + 1] for t in ring]
        ahead = [pltpu.roll(v, LANES - 1, 1) for v in taps]
        behind = [pltpu.roll(v, 1, 1) for v in taps]
        left_taps = (sub == 0) | (sub == 3) | (sub == 5)
        right_taps = (sub == 2) | (sub == 4) | (sub == 7)
        for k, t in enumerate(ring):
            after, before = ahead[k], behind[k]
            if k + 1 < size:
                after = jnp.where(lane == LANES - 1, ahead[k + 1], after)
            if k > 0:
                before = jnp.where(lane == 0, behind[k - 1], before)
            ws[t, r + 1, 0:SUB, :] = jnp.where(
                left_taps, after, jnp.where(right_taps, before, taps[k])
            )
            degree = jnp.sum(taps[k], axis=0, keepdims=True)
            ws[t, r + 1, SUB : 2 * SUB, :] = jnp.broadcast_to(degree, (SUB, LANES))

    def stencil(src, dst, rows_at, ring):
        size = len(ring)
        parts = {}

        def begin(k):
            t = ring[k]
            for at, (near_by, d, r) in enumerate(rows_at):
                tap = [
                    jnp.broadcast_to(ws[t, r + 1, pl.ds(q, 1), :], (SUB, LANES))
                    for q in range(SUB)
                ]
                degree = ws[t, r + 1, SUB : 2 * SUB, :]
                for g in range(groups):
                    part = slice(g * SUB, (g + 1) * SUB)
                    up, here, down = (src[t, e, part, :] for e in near_by)
                    parts[k, at, g] = (
                        degree * here + tap[1] * up + tap[6] * down,
                        pltpu.roll(tap[0] * up + tap[3] * here + tap[5] * down, 1, 1),
                        pltpu.roll(tap[2] * up + tap[4] * here + tap[7] * down, LANES - 1, 1),
                    )

        def end(k):
            for at, (_, d, r) in enumerate(rows_at):
                for g in range(groups):
                    center, low, high = parts[k, at, g]
                    if k > 0:
                        low = jnp.where(lane == 0, parts[k - 1, at, g][1], low)
                    if k + 1 < size:
                        high = jnp.where(lane == LANES - 1, parts[k + 1, at, g][2], high)
                    dst[ring[k], d, g * SUB : (g + 1) * SUB, :] = center + low + high

        return begin, end

    def whole_rows(src, dst, rows_at, ring):
        for row_at in rows_at:
            begin, end = stencil(src, dst, [row_at], ring)
            for k in range(len(ring)):
                begin(k)
                if k > 0:
                    end(k - 1)
            end(len(ring) - 1)

    def x_row(r):
        return {-1: 0, -2: 1, rows: rows + 3, rows + 1: rows + 2}.get(r, r + 2)

    def first_image(members):
        return [((x_row(r - 1), x_row(r), x_row(r + 1)), r + 1, r) for r in members]

    def second_image(members):
        return [((r, r + 1, r + 2), r, r) for r in members]

    def gram(src, picks):
        pieces = []
        for d, with_main, with_edge in picks:
            if with_main:
                for t in main:
                    v = src[t, d]
                    if t == 0:
                        v = jnp.where(wide_lane >= 2, v, 0.0)
                    if t == tiles - 1:
                        v = jnp.where(wide_lane < LANES - 2, v, 0.0)
                    pieces.append(v)
            if with_edge:
                pieces.append(jnp.where(wide_edge, src[edge, d], 0.0))
        both = jnp.concatenate(split(jnp.concatenate(pieces, axis=1)), axis=0)
        return lax.dot_general(both, both, NT, preferred_element_type=f32)

    wide_lane = lax.broadcasted_iota(jnp.int32, (n, LANES), 1)
    wide_edge = (wide_lane < 2) | ((wide_lane >= 62) & (wide_lane < 64))

    with jax.named_scope("weights"):
        for r in range(rows):
            shift_weights(r, main)
    with jax.named_scope("y1in"):
        whole_rows(x, y1, first_image(range(1, rows - 1)), main)
    with jax.named_scope("y2in"):
        whole_rows(y1, y2, second_image(range(2, rows - 2)), main)
    with jax.named_scope("gramin"):
        total_1 = gram(y1, [(r + 1, True, False) for r in range(1, rows - 1)])
        total_2 = gram(y2, [(r, True, False) for r in range(2, rows - 2)])

    if rounds > 1:
        with jax.named_scope("round2"):
            pl.semaphore_wait(reach.at[0], neighbours)
            if rounds > 2:
                greet(reach.at[1])

    def build_edge(kind, members, part_of):
        half, size = part_of
        both = merge(kind, half)
        for r, at in members:
            e = x_row(r)
            for g in range(groups):
                part = slice(g * SUB, (g + 1) * SUB)
                x[edge, e, part, :] = jnp.where(
                    taken, unpack(both, at * groups + g),
                    near(x[0, e, part, :], x[tiles - 1, e, part, :]),
                )
        for r, at in members:
            if -1 <= r <= rows:
                v = unpack(both, size * groups + at)
                if kind != SAME:
                    v = mirror(v)
                w[edge, r + 1] = jnp.where(taken, v, near(w[0, r + 1], w[tiles - 1, r + 1]))

    with jax.named_scope("recvnear"):
        for copy in row_copies(NEAR):
            copy.wait_recv()
    with jax.named_scope("near"):
        for t in main:
            w[t, 0] = mirror(w[t, 0])
        shift_weights(-1, main)
        whole_rows(x, y1, first_image((-1, 0)), main)
        whole_rows(y1, y2, second_image((0, 1)), main)
        total_1 = total_1 + gram(y1, [(1, True, False)])
        total_2 = total_2 + gram(y2, [(r, True, False) for r in (0, 1)])

    with jax.named_scope("recvcols"):
        for kind in (SAME, NEAR, FAR):
            for dc in (-1, 1):
                @when(kind, dc)
                def _(kind=kind, dc=dc):
                    edge_copy(kind, -dc).wait_recv()

        @when(FAR, 0)
        def _():
            row_copies(FAR, (0,))[0].wait_recv()
    with jax.named_scope("edges"):
        for h, members in enumerate(halves):
            build_edge(SAME, [(r, at) for at, r in enumerate(members)], (h, len(members)))
        build_edge(NEAR, [(-1, 0), (-2, 1)], (0, len(outer)))
        for r in range(-1, rows):
            shift_weights(r, [edge])
        for t in main:
            w[t, rows + 1] = mirror(w[t, rows + 1])
        both = merge(FAR, 0)
        v = mirror(unpack(both, len(outer) * groups + 3))
        w[edge, rows + 1] = jnp.where(taken, v, near(w[0, rows + 1], w[tiles - 1, rows + 1]))
        for ring in (main, [edge]):
            shift_weights(rows, ring)
        whole_rows(x, y1, first_image(range(-1, rows - 1)), [edge])
        whole_rows(y1, y2, second_image(range(rows - 2)), [edge])
        total_1 = total_1 + gram(y1, [(r + 1, False, True) for r in range(rows - 1)])
        total_2 = total_2 + gram(y2, [(r, False, True) for r in range(rows - 2)])

    with jax.named_scope("recvfar2"):
        @when(FAR, 0)
        def _():
            for copy in row_copies(FAR, range(1, tiles + 1)):
                copy.wait_recv()
    with jax.named_scope("far2"):
        for r, at in ((rows, 3), (rows + 1, 2)):
            e = x_row(r)
            for g in range(groups):
                part = slice(g * SUB, (g + 1) * SUB)
                x[edge, e, part, :] = jnp.where(
                    taken, unpack(both, at * groups + g),
                    near(x[0, e, part, :], x[tiles - 1, e, part, :]),
                )
        for ring in (main, [edge]):
            whole_rows(x, y1, first_image((rows - 1, rows)), ring)
        for ring in (main, [edge]):
            whole_rows(y1, y2, second_image((rows - 2, rows - 1)), ring)
        total_1 = total_1 + gram(y1, [(rows, True, True)])
        total_2 = total_2 + gram(y2, [(r, True, True) for r in (rows - 2, rows - 1)])

    scale = 1.0 / (rows * cols * R * C)

    def fold(total):
        half = total[0:n] + total[n : 2 * n]
        square = (half[:, 0:n] + half[:, n : 2 * n]) * scale
        return jnp.concatenate([square[g * SUB : (g + 1) * SUB] for g in range(groups)], axis=1)

    def gather_copies(stage, receiving):
        axes, count = stages[stage]
        me = {"row": i, "col": j, "both": j * R + i}[axes]
        copies = []
        for k in range(count - 1):
            peer = k + (k >= me).astype(jnp.int32)
            slot = peer if receiving else me
            target = {
                "row": {"row": peer, "col": j},
                "col": {"row": i, "col": peer},
                "both": {"row": lax.rem(peer, R), "col": lax.div(peer, R)},
            }[axes]
            copies.append(pltpu.make_async_remote_copy(
                src_ref=sent.at[stage], dst_ref=held.at[stage, slot],
                send_sem=gather_send.at[stage, k],
                recv_sem=gather_recv.at[stage, slot],
                device_id=target, device_id_type=MESH,
            ))
        return copies

    def spread(stage, value, diagonal):
        axes, count = stages[stage]
        me = {"row": i, "col": j, "both": j * R + i}[axes]
        for ref in (sent.at[stage], held.at[stage, me]):
            ref[0:SUB, :] = value
            ref[SUB : SUB + 1, :] = diagonal
        for copy in gather_copies(stage, False):
            copy.start()

    def collect(stage):
        for copy in gather_copies(stage, True):
            copy.wait_recv()
        totals = []
        for part in (slice(0, SUB), slice(SUB, SUB + 1)):
            terms = [held[stage, at, part, :] for at in range(stages[stage][1])]
            while len(terms) > 1:
                terms = [sum(terms[k + 1 : k + 2], terms[k]) for k in range(0, len(terms), 2)]
            totals.append(terms[0])
        return totals

    with jax.named_scope("fold"):
        across, down = lane % n, sub + SUB * (lane // n)
        folded = fold(total_2)
        value = jnp.where(across >= down, fold(total_1), folded)
        diagonal = jnp.sum(jnp.where(across == down, folded, 0.0), axis=0, keepdims=True)
    for k in range(2, rounds):
        with jax.named_scope("round3"):
            pl.semaphore_wait(reach.at[k - 1], neighbours)
            if k + 1 < rounds:
                greet(reach.at[k])
    with jax.named_scope("spread"):
        spread(0, value, diagonal)

    def eliminate(square, diagonal, step=SUB):
        blocks = []
        half = lane % 64
        stacked = jnp.concatenate(
            [square] + [pltpu.roll(square, LANES - g * n, 1) for g in range(1, groups)], axis=0
        )
        turned = stacked.T[0:n]
        diagonal = jnp.broadcast_to(diagonal, (SUB, LANES))
        for g in range(groups):
            part = slice(g * SUB, (g + 1) * SUB)
            row = sub + g * SUB
            mirror = jnp.concatenate([turned[part]] * (LANES // n), axis=1)
            whole = jnp.concatenate([stacked[part, 0:n]] * (LANES // n), axis=1)
            shifted = pltpu.roll(diagonal, (64 - g * n) % LANES, 1)
            first = jnp.where(lane >= row, whole, mirror)
            second = jnp.where(half < row, whole, jnp.where(half == row, shifted, mirror))
            eye = (half - n == row).astype(f32)
            blocks.append(jnp.where(half < n, jnp.where(lane < 64, first, second), eye))

        def over_lanes(v, p):
            return jnp.where(
                lane < 64,
                jnp.broadcast_to(v[:, p : p + 1], (SUB, LANES)),
                jnp.broadcast_to(v[:, 64 + p : 64 + p + 1], (SUB, LANES)),
            )

        solved = [jnp.zeros((SUB, LANES), f32)] * groups
        for p in range(0, n, step):
            home, base = p // SUB, p % SUB
            line = [
                jnp.broadcast_to(blocks[home][base + q : base + q + 1, :], (SUB, LANES))
                for q in range(step)
            ]
            column = {
                (s, g): over_lanes(blocks[g], p + s)
                for g in range(home, groups)
                for s in range(step)
            }
            corner = {
                (q, s): jnp.broadcast_to(column[s, home][base + q : base + q + 1, :], (SUB, LANES))
                for q in range(step)
                for s in range(q, step)
            }
            scaled = []
            for q in range(step):
                over = 1.0 / corner[q, q]
                scaled.append(line[q] * over)
                ratio = {s: corner[q, s] * over for s in range(q + 1, step)}
                for s in range(q + 1, step):
                    line[s] = line[s] - ratio[s] * line[q]
                    for t in range(s, step):
                        corner[s, t] = corner[s, t] - ratio[s] * corner[q, t]
                    for g in range(home + (base + step == SUB), groups):
                        column[s, g] = column[s, g] - ratio[s] * column[q, g]
            for g in range(home + (base + step == SUB), groups):
                update = column[0, g] * scaled[0]
                for q in range(1, step):
                    update = update + column[q, g] * scaled[q]
                blocks[g] = blocks[g] - update
            for q in range(step):
                done = line[q] * lax.rsqrt(corner[q, q])
                solved[home] = jnp.where(sub == base + q, done, solved[home])
        return jnp.concatenate(solved, axis=0)

    for stage in range(1, len(stages)):
        spread(stage, *collect(stage - 1))
    with jax.named_scope("patch"):
        for r in range(rows):
            edges = y2[edge, r]
            pieces = [y2[t, r] for t in main]
            pieces[0] = jnp.where(wide_lane < 2, edges, pieces[0])
            pieces[-1] = jnp.where(wide_lane >= LANES - 2, pltpu.roll(edges, 64, 1), pieces[-1])
            y2_out[original(r)] = jnp.concatenate(split(jnp.concatenate(pieces, axis=1)), axis=0)
    with jax.named_scope("collect"):
        square, diagonal = collect(len(stages) - 1)
    with jax.named_scope("eliminate"):
        tables[...] = eliminate(square, diagonal)

    with jax.named_scope("drain"):
        for kind, dc in around:
            @when(kind, dc)
            def _(kind=kind, dc=dc):
                edge_copy(kind, dc).wait_send()
        for kind in (NEAR, FAR):
            @when(kind, 0)
            def _(kind=kind):
                for copy in row_copies(kind):
                    copy.wait_send()
        for stage in range(len(stages)):
            for copy in gather_copies(stage, False):
                copy.wait_send()


def finish(n, rows, cols, y2, tables, out_ref, fac_ref, staged, fac, store_sem):
    groups = n // SUB
    tiles = cols // LANES
    inv_hi, inv_lo = split(tables[:, 3 * n : 4 * n])
    left = jnp.concatenate([inv_hi, inv_lo, inv_hi], axis=1)
    stores = []
    for t0 in range(0, tiles, 2):
        for r in range(rows):
            hi = y2[r, 0:n, t0 * LANES : (t0 + 2) * LANES]
            lo = y2[r, n : 2 * n, t0 * LANES : (t0 + 2) * LANES]
            right = jnp.concatenate([hi, hi, lo], axis=0)
            solved = jnp.dot(left, right, preferred_element_type=f32)
            for t in range(2):
                for g in range(groups):
                    staged[t0 + t, pl.ds(g * SUB * rows + r, SUB, stride=rows), :] = solved[
                        g * SUB : (g + 1) * SUB, t * LANES : (t + 1) * LANES
                    ]
        for t in range(t0, t0 + 2):
            stores.append(pltpu.make_async_copy(
                staged.at[t], out_ref.at[:, pl.ds(t * LANES, LANES)], store_sem.at[t]
            ))
            stores[-1].start()
    inverse_1 = tables[:, n : 2 * n]
    upper_2 = tables[:, 2 * n : 3 * n]
    row_at = lax.broadcasted_iota(jnp.int32, (n, n), 0)
    col_at = lax.broadcasted_iota(jnp.int32, (n, n), 1)
    upper_2 = jnp.where(col_at >= row_at, upper_2, 0.0)
    last = lax.dot_general(upper_2, inverse_1, NT, precision=HIGHEST, preferred_element_type=f32)
    fac[...] = jnp.where(col_at >= row_at, last, 0.0)
    stores.append(pltpu.make_async_copy(fac, fac_ref, store_sem.at[tiles]))
    stores[-1].start()
    with jax.named_scope("storewait"):
        for store in stores:
            store.wait()


def on_device(sketch, weights):
    n, rows, cols = sketch.shape
    R, C = lax.axis_size("row"), lax.axis_size("col")
    tiles = cols // LANES
    stages = (("both", R * C),) if R * C <= 16 else (("row", R), ("col", C))
    rounds = max(R, C) - 1
    peers = max(count for _, count in stages)
    dma = pltpu.SemaphoreType.DMA
    image, tables = pl.pallas_call(
        functools.partial(kernel, n, rows, cols, R, C, stages, rounds),
        out_shape=(
            pltpu.VMEM((rows, 2 * n, cols), bf16),
            pltpu.VMEM((n, LANES), f32),
        ),
        in_specs=[pl.BlockSpec(memory_space=pltpu.HBM)] * 2,
        out_specs=(
            pl.BlockSpec(memory_space=pltpu.VMEM),
            pl.BlockSpec(memory_space=pltpu.VMEM),
        ),
        scratch_shapes=[
            pltpu.VMEM((tiles, n * rows, LANES), f32),
            pltpu.VMEM((tiles, SUB * rows, LANES), f32),
            pltpu.VMEM((tiles + 1, rows + 4, n, LANES), f32),
            pltpu.VMEM((tiles + 1, rows + 2, SUB, LANES), f32),
            pltpu.VMEM((tiles + 1, rows + 2, 2 * SUB, LANES), f32),
            pltpu.VMEM((tiles + 1, rows + 2, n, LANES), f32),
            pltpu.VMEM((tiles + 1, rows, n, LANES), f32),
            pltpu.VMEM((2 * SUB, LANES), f32),
            pltpu.VMEM((6, 2 * SUB, LANES), f32),
            pltpu.VMEM((len(stages), peers, SUB + 1, LANES), f32),
            pltpu.VMEM((len(stages), SUB + 1, LANES), f32),
            dma((2, tiles)), dma((6,)), dma((6,)), dma((2, tiles + 1)), dma((2, tiles + 1)),
            dma((len(stages), peers)), dma((len(stages), peers)),
            pltpu.SemaphoreType.REGULAR((max(rounds - 1, 1),)),
        ],
        compiler_params=pltpu.CompilerParams(
            collective_id=0, has_side_effects=True, vmem_limit_bytes=16 * 1024 * 1024
        ),
    )(
        pltpu.with_memory_space_constraint(sketch.reshape(n * rows, cols), pltpu.HBM),
        pltpu.with_memory_space_constraint(weights.reshape(SUB * rows, cols), pltpu.HBM),
    )
    basis, factor = pl.pallas_call(
        functools.partial(finish, n, rows, cols),
        out_shape=(
            jax.ShapeDtypeStruct((n * rows, cols), f32),
            jax.ShapeDtypeStruct((n, n), f32),
        ),
        in_specs=[pl.BlockSpec(memory_space=pltpu.VMEM)] * 2,
        out_specs=(
            pl.BlockSpec(memory_space=pl.ANY),
            pl.BlockSpec(memory_space=pl.ANY),
        ),
        scratch_shapes=[
            pltpu.VMEM((tiles, n * rows, LANES), f32),
            pltpu.VMEM((n, n), f32),
            dma((tiles + 1,)),
        ],
        compiler_params=pltpu.CompilerParams(vmem_limit_bytes=16 * 1024 * 1024),
    )(image, tables)
    return basis.reshape(n, rows, cols), factor


def solution(mesh):
    return jax.shard_map(
        on_device,
        mesh=mesh,
        in_specs=(P(None, ("sec", "row"), "col"), P(None, ("sec", "row"), "col")),
        out_specs=(P(None, ("sec", "row"), "col"), P("sec", None)),
        check_vma=False,
    )
```

```python
import functools

import jax
import jax.numpy as jnp
from jax import lax
from jax.experimental import pallas as pl
from jax.experimental.pallas import tpu as pltpu
from jax.sharding import PartitionSpec as P

LANES = 128
SUB = 8
MESH = pl.DeviceIdType.MESH
NT = (((1,), (1,)), ((), ()))
HIGHEST = lax.Precision.HIGHEST
f32 = jnp.float32
bf16 = jnp.bfloat16


def split(x):
    hi = x.astype(bf16)
    lo = (x - hi.astype(f32)).astype(bf16)
    return hi, lo


def kernel(
    n, rows, cols, R, C, stages, rounds,
    sk_hbm, w_hbm, y2_out, tables,
    raw, wraw, x, w, ws, y1, y2, pack, nb, held, sent,
    load_sem, col_send, col_recv, row_send, row_recv, gather_send, gather_recv, reach,
):
    groups = n // SUB
    tiles = cols // LANES
    i = lax.axis_index("row")
    j = lax.axis_index("col")
    flip = 1 - lax.rem(i, 2)
    near_i = i + 2 * flip - 1
    far_i = i + 1 - 2 * flip
    has_far = (far_i >= 0) & (far_i < R)
    has_left, has_right = j > 0, j < C - 1

    kinds = ((i, None), (near_i, None), (far_i, has_far))
    SAME, NEAR, FAR = range(3)
    sides = {-1: has_left, 0: None, 1: has_right}
    beside = [(FAR, 0), (NEAR, 0)]
    around = [(kind, dc) for kind in (SAME, FAR, NEAR) for dc in (-1, 1)]

    def when(kind, dc):
        terms = [t for t in (kinds[kind][1], sides[dc]) if t is not None]
        if not terms:
            return lambda body: body()
        return pl.when(functools.reduce(jnp.logical_and, terms))

    def unless(kind, dc):
        terms = [t for t in (kinds[kind][1], sides[dc]) if t is not None]
        if not terms:
            return lambda body: None
        return pl.when(jnp.logical_not(functools.reduce(jnp.logical_and, terms)))

    def at_offset(kind, dc):
        return {"row": kinds[kind][0], "col": j + dc}

    def greet(sem):
        for kind, dc in beside + around:
            @when(kind, dc)
            def _(kind=kind, dc=dc):
                pl.semaphore_signal(sem, inc=1, device_id=at_offset(kind, dc), device_id_type=MESH)

    height = 2 + has_far.astype(jnp.int32)
    breadth = 1 + has_left.astype(jnp.int32) + has_right.astype(jnp.int32)
    neighbours = height * breadth - 1

    barrier = pltpu.get_barrier_semaphore()
    greet(barrier)

    loads = []
    for t in range(tiles):
        across = pl.ds(t * LANES, LANES)
        loads.append(pltpu.make_async_copy(sk_hbm.at[:, across], raw.at[t], load_sem.at[0, t]))
        loads.append(pltpu.make_async_copy(w_hbm.at[:, across], wraw.at[t], load_sem.at[1, t]))
    for load in loads:
        load.start()

    lane = lax.broadcasted_iota(jnp.int32, (SUB, LANES), 1)
    sub = lax.broadcasted_iota(jnp.int32, (SUB, LANES), 0)

    for load in loads:
        load.wait()
    def mirror(v):
        return jnp.where(
            sub < 3, pltpu.roll(v, 3, 0), jnp.where(sub < 5, v, pltpu.roll(v, 5, 0))
        )

    def original(r):
        return r + flip * (rows - 1 - 2 * r)

    def relayout(members):
        for r in members:
            r0 = original(r)
            for t in range(tiles):
                for g in range(groups):
                    x[t, r + 2, g * SUB : (g + 1) * SUB, :] = raw[
                        t, pl.ds(g * SUB * rows + r0, SUB, stride=rows), :
                    ]
                v = wraw[t, pl.ds(r0, SUB, stride=rows), :]
                w[t, r + 1] = jnp.where(flip == 1, mirror(v), v)

    outer = [0, 1, rows - 2, rows - 1]
    inner = list(range(2, rows - 2))
    halves = (outer, inner)

    def edge_copy(kind, dc):
        at = 2 * kind + (0 if dc > 0 else 1)
        size = 2 * SUB if kind == SAME else SUB
        return pltpu.make_async_remote_copy(
            src_ref=pack.at[pl.ds(0, size)], dst_ref=nb.at[at, pl.ds(0, size)],
            send_sem=col_send.at[at], recv_sem=col_recv.at[at],
            device_id=at_offset(kind, dc), device_id_type=MESH,
        )

    def row_copies(kind, only=None):
        at = 0 if kind == NEAR else 1
        refs = [(
            w.at[pl.ds(0, tiles), 1 if kind == NEAR else rows],
            w.at[pl.ds(0, tiles), 0 if kind == NEAR else rows + 1],
        )]
        src, dst = (2, 0) if kind == NEAR else (rows, rows + 2)
        for t in range(tiles):
            refs.append((x.at[t, pl.ds(src, 2)], x.at[t, pl.ds(dst, 2)]))
        return [
            pltpu.make_async_remote_copy(
                src_ref=a, dst_ref=b, send_sem=row_send.at[at, k], recv_sem=row_recv.at[at, k],
                device_id=at_offset(kind, 0), device_id_type=MESH,
            )
            for k, (a, b) in enumerate(refs)
            if only is None or k in only
        ]

    relayout(range(rows))
    for h, members in enumerate(halves):
        packed = jnp.zeros((SUB, LANES), f32)
        for at, r in enumerate(members):
            for g in range(groups + 1):
                if g < groups:
                    slot = at * groups + g
                    first = x[0, r + 2, g * SUB : (g + 1) * SUB, :]
                    final = x[tiles - 1, r + 2, g * SUB : (g + 1) * SUB, :]
                else:
                    slot = len(members) * groups + at
                    first, final = w[0, r + 1], w[tiles - 1, r + 1]
                edge = jnp.where(lane < LANES // 2, first, final)
                moved = pltpu.roll(edge, (4 * slot + 2) % LANES, 1)
                packed = jnp.where(lane // 4 == slot, moved, packed)
        pack[h * SUB : (h + 1) * SUB, :] = packed
    pl.semaphore_wait(barrier, neighbours)
    for kind, dc in around:
        @when(kind, dc)
        def _(kind=kind, dc=dc):
            edge_copy(kind, dc).start()
    for kind in (FAR, NEAR):
        @when(kind, 0)
        def _(kind=kind):
            for copy in row_copies(kind):
                copy.start()
    if rounds > 1:
        greet(reach.at[0])

    @unless(FAR, 0)
    def _():
        for t in range(tiles):
            x[t, rows + 2 : rows + 4] = jnp.zeros((2, n, LANES), f32)
            w[t, rows + 1] = jnp.zeros((SUB, LANES), f32)

    for kind, dc in around:
        @unless(kind, dc)
        def _(kind=kind, dc=dc):
            nb[2 * kind + (1 if dc > 0 else 0)] = jnp.zeros((2 * SUB, LANES), f32)

    edge = tiles
    main = list(range(tiles))
    taken = (lane >= LANES - 2) | ((lane >= 64) & (lane < 66))

    def merge(kind, h):
        at = 2 * kind
        part = pl.ds(h * SUB, SUB)
        return jnp.where(lane % 4 < 2, nb[at, part, :], pltpu.roll(nb[at + 1, part, :], 64, 1))

    def unpack(both, slot):
        return pltpu.roll(both, (-(4 * slot + 2)) % LANES, 1)

    def near(first, final):
        return jnp.where((lane >= 32) & (lane < 96), pltpu.roll(final, 64, 1), first)

    def shift_weights(r, ring):
        size = len(ring)
        taps = [w[t, r + 1] for t in ring]
        ahead = [pltpu.roll(v, LANES - 1, 1) for v in taps]
        behind = [pltpu.roll(v, 1, 1) for v in taps]
        left_taps = (sub == 0) | (sub == 3) | (sub == 5)
        right_taps = (sub == 2) | (sub == 4) | (sub == 7)
        for k, t in enumerate(ring):
            after, before = ahead[k], behind[k]
            if k + 1 < size:
                after = jnp.where(lane == LANES - 1, ahead[k + 1], after)
            if k > 0:
                before = jnp.where(lane == 0, behind[k - 1], before)
            ws[t, r + 1, 0:SUB, :] = jnp.where(
                left_taps, after, jnp.where(right_taps, before, taps[k])
            )
            degree = jnp.sum(taps[k], axis=0, keepdims=True)
            ws[t, r + 1, SUB : 2 * SUB, :] = jnp.broadcast_to(degree, (SUB, LANES))

    def stencil(src, dst, rows_at, ring):
        size = len(ring)
        parts = {}

        def begin(k):
            t = ring[k]
            for at, (near_by, d, r) in enumerate(rows_at):
                tap = [
                    jnp.broadcast_to(ws[t, r + 1, pl.ds(q, 1), :], (SUB, LANES))
                    for q in range(SUB)
                ]
                degree = ws[t, r + 1, SUB : 2 * SUB, :]
                for g in range(groups):
                    part = slice(g * SUB, (g + 1) * SUB)
                    up, here, down = (src[t, e, part, :] for e in near_by)
                    parts[k, at, g] = (
                        degree * here + tap[1] * up + tap[6] * down,
                        pltpu.roll(tap[0] * up + tap[3] * here + tap[5] * down, 1, 1),
                        pltpu.roll(tap[2] * up + tap[4] * here + tap[7] * down, LANES - 1, 1),
                    )

        def end(k):
            for at, (_, d, r) in enumerate(rows_at):
                for g in range(groups):
                    center, low, high = parts[k, at, g]
                    if k > 0:
                        low = jnp.where(lane == 0, parts[k - 1, at, g][1], low)
                    if k + 1 < size:
                        high = jnp.where(lane == LANES - 1, parts[k + 1, at, g][2], high)
                    dst[ring[k], d, g * SUB : (g + 1) * SUB, :] = center + low + high

        return begin, end

    def whole_rows(src, dst, rows_at, ring):
        for row_at in rows_at:
            begin, end = stencil(src, dst, [row_at], ring)
            for k in range(len(ring)):
                begin(k)
                if k > 0:
                    end(k - 1)
            end(len(ring) - 1)

    def x_row(r):
        return {-1: 0, -2: 1, rows: rows + 3, rows + 1: rows + 2}.get(r, r + 2)

    def first_image(members):
        return [((x_row(r - 1), x_row(r), x_row(r + 1)), r + 1, r) for r in members]

    def second_image(members):
        return [((r, r + 1, r + 2), r, r) for r in members]

    def gram(src, picks):
        pieces = []
        for d, with_main, with_edge in picks:
            if with_main:
                for t in main:
                    v = src[t, d]
                    if t == 0:
                        v = jnp.where(wide_lane >= 2, v, 0.0)
                    if t == tiles - 1:
                        v = jnp.where(wide_lane < LANES - 2, v, 0.0)
                    pieces.append(v)
            if with_edge:
                pieces.append(jnp.where(wide_edge, src[edge, d], 0.0))
        both = jnp.concatenate(split(jnp.concatenate(pieces, axis=1)), axis=0)
        return lax.dot_general(both, both, NT, preferred_element_type=f32)

    wide_lane = lax.broadcasted_iota(jnp.int32, (n, LANES), 1)
    wide_edge = (wide_lane < 2) | ((wide_lane >= 62) & (wide_lane < 64))

    for r in range(rows):
        shift_weights(r, main)
    whole_rows(x, y1, first_image(range(1, rows - 1)), main)
    whole_rows(y1, y2, second_image(range(2, rows - 2)), main)
    total_1 = gram(y1, [(r + 1, True, False) for r in range(1, rows - 1)])
    total_2 = gram(y2, [(r, True, False) for r in range(2, rows - 2)])

    if rounds > 1:
        pl.semaphore_wait(reach.at[0], neighbours)
        if rounds > 2:
            greet(reach.at[1])

    def build_edge(kind, members, part_of):
        half, size = part_of
        both = merge(kind, half)
        for r, at in members:
            e = x_row(r)
            for g in range(groups):
                part = slice(g * SUB, (g + 1) * SUB)
                x[edge, e, part, :] = jnp.where(
                    taken, unpack(both, at * groups + g),
                    near(x[0, e, part, :], x[tiles - 1, e, part, :]),
                )
        for r, at in members:
            if -1 <= r <= rows:
                v = unpack(both, size * groups + at)
                if kind != SAME:
                    v = mirror(v)
                w[edge, r + 1] = jnp.where(taken, v, near(w[0, r + 1], w[tiles - 1, r + 1]))

    for copy in row_copies(NEAR):
        copy.wait_recv()
    for t in main:
        w[t, 0] = mirror(w[t, 0])
    shift_weights(-1, main)
    whole_rows(x, y1, first_image((-1, 0)), main)
    whole_rows(y1, y2, second_image((0, 1)), main)
    total_1 = total_1 + gram(y1, [(1, True, False)])
    total_2 = total_2 + gram(y2, [(r, True, False) for r in (0, 1)])

    for kind in (SAME, NEAR, FAR):
        for dc in (-1, 1):
            @when(kind, dc)
            def _(kind=kind, dc=dc):
                edge_copy(kind, -dc).wait_recv()

    @when(FAR, 0)
    def _():
        row_copies(FAR, (0,))[0].wait_recv()
    for h, members in enumerate(halves):
        build_edge(SAME, [(r, at) for at, r in enumerate(members)], (h, len(members)))
    build_edge(NEAR, [(-1, 0), (-2, 1)], (0, len(outer)))
    for r in range(-1, rows):
        shift_weights(r, [edge])
    for t in main:
        w[t, rows + 1] = mirror(w[t, rows + 1])
    both = merge(FAR, 0)
    v = mirror(unpack(both, len(outer) * groups + 3))
    w[edge, rows + 1] = jnp.where(taken, v, near(w[0, rows + 1], w[tiles - 1, rows + 1]))
    for ring in (main, [edge]):
        shift_weights(rows, ring)
    whole_rows(x, y1, first_image(range(-1, rows - 1)), [edge])
    whole_rows(y1, y2, second_image(range(rows - 2)), [edge])
    total_1 = total_1 + gram(y1, [(r + 1, False, True) for r in range(rows - 1)])
    total_2 = total_2 + gram(y2, [(r, False, True) for r in range(rows - 2)])

    @when(FAR, 0)
    def _():
        for copy in row_copies(FAR, range(1, tiles + 1)):
            copy.wait_recv()
    for r, at in ((rows, 3), (rows + 1, 2)):
        e = x_row(r)
        for g in range(groups):
            part = slice(g * SUB, (g + 1) * SUB)
            x[edge, e, part, :] = jnp.where(
                taken, unpack(both, at * groups + g),
                near(x[0, e, part, :], x[tiles - 1, e, part, :]),
            )
    for ring in (main, [edge]):
        whole_rows(x, y1, first_image((rows - 1, rows)), ring)
    total_1 = total_1 + gram(y1, [(rows, True, True)])
    for ring in (main, [edge]):
        whole_rows(y1, y2, second_image((rows - 2, rows - 1)), ring)
    total_2 = total_2 + gram(y2, [(r, True, True) for r in (rows - 2, rows - 1)])

    scale = 1.0 / (rows * cols * R * C)

    def fold(total):
        half = total[0:n] + total[n : 2 * n]
        square = (half[:, 0:n] + half[:, n : 2 * n]) * scale
        return jnp.concatenate([square[g * SUB : (g + 1) * SUB] for g in range(groups)], axis=1)

    def gather_copies(stage, receiving):
        axes, count = stages[stage]
        me = {"row": i, "col": j, "both": j * R + i}[axes]
        copies = []
        for k in range(count - 1):
            peer = k + (k >= me).astype(jnp.int32)
            slot = peer if receiving else me
            target = {
                "row": {"row": peer, "col": j},
                "col": {"row": i, "col": peer},
                "both": {"row": lax.rem(peer, R), "col": lax.div(peer, R)},
            }[axes]
            copies.append(pltpu.make_async_remote_copy(
                src_ref=sent.at[stage], dst_ref=held.at[stage, slot],
                send_sem=gather_send.at[stage, k],
                recv_sem=gather_recv.at[stage, slot],
                device_id=target, device_id_type=MESH,
            ))
        return copies

    def spread(stage, value, diagonal):
        axes, count = stages[stage]
        me = {"row": i, "col": j, "both": j * R + i}[axes]
        for ref in (sent.at[stage], held.at[stage, me]):
            ref[0:SUB, :] = value
            ref[SUB : SUB + 1, :] = diagonal
        for copy in gather_copies(stage, False):
            copy.start()

    def collect(stage):
        for copy in gather_copies(stage, True):
            copy.wait_recv()
        totals = []
        for part in (slice(0, SUB), slice(SUB, SUB + 1)):
            terms = [held[stage, at, part, :] for at in range(stages[stage][1])]
            while len(terms) > 1:
                terms = [sum(terms[k + 1 : k + 2], terms[k]) for k in range(0, len(terms), 2)]
            totals.append(terms[0])
        return totals

    across, down = lane % n, sub + SUB * (lane // n)
    folded = fold(total_2)
    value = jnp.where(across >= down, fold(total_1), folded)
    diagonal = jnp.sum(jnp.where(across == down, folded, 0.0), axis=0, keepdims=True)
    for k in range(2, rounds):
        pl.semaphore_wait(reach.at[k - 1], neighbours)
        if k + 1 < rounds:
            greet(reach.at[k])
    spread(0, value, diagonal)

    def eliminate(square, diagonal, step=SUB):
        blocks = []
        half = lane % 64
        stacked = jnp.concatenate(
            [square] + [pltpu.roll(square, LANES - g * n, 1) for g in range(1, groups)], axis=0
        )
        turned = stacked.T[0:n]
        diagonal = jnp.broadcast_to(diagonal, (SUB, LANES))
        for g in range(groups):
            part = slice(g * SUB, (g + 1) * SUB)
            row = sub + g * SUB
            mirror = jnp.concatenate([turned[part]] * (LANES // n), axis=1)
            whole = jnp.concatenate([stacked[part, 0:n]] * (LANES // n), axis=1)
            shifted = pltpu.roll(diagonal, (64 - g * n) % LANES, 1)
            first = jnp.where(lane >= row, whole, mirror)
            second = jnp.where(half < row, whole, jnp.where(half == row, shifted, mirror))
            eye = (half - n == row).astype(f32)
            blocks.append(jnp.where(half < n, jnp.where(lane < 64, first, second), eye))

        def over_lanes(v, p):
            return jnp.where(
                lane < 64,
                jnp.broadcast_to(v[:, p : p + 1], (SUB, LANES)),
                jnp.broadcast_to(v[:, 64 + p : 64 + p + 1], (SUB, LANES)),
            )

        solved = [jnp.zeros((SUB, LANES), f32)] * groups
        for p in range(0, n, step):
            home, base = p // SUB, p % SUB
            line = [
                jnp.broadcast_to(blocks[home][base + q : base + q + 1, :], (SUB, LANES))
                for q in range(step)
            ]
            column = {
                (s, g): over_lanes(blocks[g], p + s)
                for g in range(home, groups)
                for s in range(step)
            }
            corner = {
                (q, s): jnp.broadcast_to(column[s, home][base + q : base + q + 1, :], (SUB, LANES))
                for q in range(step)
                for s in range(q, step)
            }
            scaled = []
            for q in range(step):
                over = 1.0 / corner[q, q]
                scaled.append(line[q] * over)
                ratio = {s: corner[q, s] * over for s in range(q + 1, step)}
                for s in range(q + 1, step):
                    line[s] = line[s] - ratio[s] * line[q]
                    for t in range(s, step):
                        corner[s, t] = corner[s, t] - ratio[s] * corner[q, t]
                    for g in range(home + (base + step == SUB), groups):
                        column[s, g] = column[s, g] - ratio[s] * column[q, g]
            for g in range(home + (base + step == SUB), groups):
                update = column[0, g] * scaled[0]
                for q in range(1, step):
                    update = update + column[q, g] * scaled[q]
                blocks[g] = blocks[g] - update
            for q in range(step):
                done = line[q] * lax.rsqrt(corner[q, q])
                solved[home] = jnp.where(sub == base + q, done, solved[home])
        return jnp.concatenate(solved, axis=0)

    for stage in range(1, len(stages)):
        spread(stage, *collect(stage - 1))
    for r in range(rows):
        edges = y2[edge, r]
        pieces = [y2[t, r] for t in main]
        pieces[0] = jnp.where(wide_lane < 2, edges, pieces[0])
        pieces[-1] = jnp.where(wide_lane >= LANES - 2, pltpu.roll(edges, 64, 1), pieces[-1])
        y2_out[original(r)] = jnp.concatenate(split(jnp.concatenate(pieces, axis=1)), axis=0)
    for kind, dc in around:
        @when(kind, dc)
        def _(kind=kind, dc=dc):
            edge_copy(kind, dc).wait_send()
    for kind in (NEAR, FAR):
        @when(kind, 0)
        def _(kind=kind):
            for copy in row_copies(kind):
                copy.wait_send()

    square, diagonal = collect(len(stages) - 1)
    tables[...] = eliminate(square, diagonal)

    for stage in range(len(stages)):
        for copy in gather_copies(stage, False):
            copy.wait_send()


def finish(n, rows, cols, y2, tables, out_ref, fac_ref, staged, fac, store_sem):
    groups = n // SUB
    tiles = cols // LANES
    inv_hi, inv_lo = split(tables[:, 3 * n : 4 * n])
    left = jnp.concatenate([inv_hi, inv_lo, inv_hi], axis=1)
    stores = []
    for t0 in range(0, tiles, 2):
        for r in range(rows):
            hi = y2[r, 0:n, t0 * LANES : (t0 + 2) * LANES]
            lo = y2[r, n : 2 * n, t0 * LANES : (t0 + 2) * LANES]
            right = jnp.concatenate([hi, hi, lo], axis=0)
            solved = jnp.dot(left, right, preferred_element_type=f32)
            for t in range(2):
                for g in range(groups):
                    staged[t0 + t, pl.ds(g * SUB * rows + r, SUB, stride=rows), :] = solved[
                        g * SUB : (g + 1) * SUB, t * LANES : (t + 1) * LANES
                    ]
        for t in range(t0, t0 + 2):
            stores.append(pltpu.make_async_copy(
                staged.at[t], out_ref.at[:, pl.ds(t * LANES, LANES)], store_sem.at[t]
            ))
            stores[-1].start()
    inverse_1 = tables[:, n : 2 * n]
    upper_2 = tables[:, 2 * n : 3 * n]
    row_at = lax.broadcasted_iota(jnp.int32, (n, n), 0)
    col_at = lax.broadcasted_iota(jnp.int32, (n, n), 1)
    upper_2 = jnp.where(col_at >= row_at, upper_2, 0.0)
    last = lax.dot_general(upper_2, inverse_1, NT, precision=HIGHEST, preferred_element_type=f32)
    fac[...] = jnp.where(col_at >= row_at, last, 0.0)
    stores.append(pltpu.make_async_copy(fac, fac_ref, store_sem.at[tiles]))
    stores[-1].start()
    for store in stores:
        store.wait()


def on_device(sketch, weights):
    n, rows, cols = sketch.shape
    R, C = lax.axis_size("row"), lax.axis_size("col")
    tiles = cols // LANES
    stages = (("both", R * C),) if R * C <= 16 else (("row", R), ("col", C))
    rounds = max(R, C) - 1
    peers = max(count for _, count in stages)
    dma = pltpu.SemaphoreType.DMA
    image, tables = pl.pallas_call(
        functools.partial(kernel, n, rows, cols, R, C, stages, rounds),
        out_shape=(
            pltpu.VMEM((rows, 2 * n, cols), bf16),
            pltpu.VMEM((n, LANES), f32),
        ),
        in_specs=[pl.BlockSpec(memory_space=pltpu.HBM)] * 2,
        out_specs=(
            pl.BlockSpec(memory_space=pltpu.VMEM),
            pl.BlockSpec(memory_space=pltpu.VMEM),
        ),
        scratch_shapes=[
            pltpu.VMEM((tiles, n * rows, LANES), f32),
            pltpu.VMEM((tiles, SUB * rows, LANES), f32),
            pltpu.VMEM((tiles + 1, rows + 4, n, LANES), f32),
            pltpu.VMEM((tiles + 1, rows + 2, SUB, LANES), f32),
            pltpu.VMEM((tiles + 1, rows + 2, 2 * SUB, LANES), f32),
            pltpu.VMEM((tiles + 1, rows + 2, n, LANES), f32),
            pltpu.VMEM((tiles + 1, rows, n, LANES), f32),
            pltpu.VMEM((2 * SUB, LANES), f32),
            pltpu.VMEM((6, 2 * SUB, LANES), f32),
            pltpu.VMEM((len(stages), peers, SUB + 1, LANES), f32),
            pltpu.VMEM((len(stages), SUB + 1, LANES), f32),
            dma((2, tiles)), dma((6,)), dma((6,)), dma((2, tiles + 1)), dma((2, tiles + 1)),
            dma((len(stages), peers)), dma((len(stages), peers)),
            pltpu.SemaphoreType.REGULAR((max(rounds - 1, 1),)),
        ],
        compiler_params=pltpu.CompilerParams(
            collective_id=0, has_side_effects=True, vmem_limit_bytes=16 * 1024 * 1024
        ),
    )(
        pltpu.with_memory_space_constraint(sketch.reshape(n * rows, cols), pltpu.HBM),
        pltpu.with_memory_space_constraint(weights.reshape(SUB * rows, cols), pltpu.HBM),
    )
    basis, factor = pl.pallas_call(
        functools.partial(finish, n, rows, cols),
        out_shape=(
            jax.ShapeDtypeStruct((n * rows, cols), f32),
            jax.ShapeDtypeStruct((n, n), f32),
        ),
        in_specs=[pl.BlockSpec(memory_space=pltpu.VMEM)] * 2,
        out_specs=(
            pl.BlockSpec(memory_space=pl.ANY),
            pl.BlockSpec(memory_space=pl.ANY),
        ),
        scratch_shapes=[
            pltpu.VMEM((tiles, n * rows, LANES), f32),
            pltpu.VMEM((n, n), f32),
            dma((tiles + 1,)),
        ],
        compiler_params=pltpu.CompilerParams(vmem_limit_bytes=16 * 1024 * 1024),
    )(image, tables)
    return basis.reshape(n, rows, cols), factor


def solution(mesh):
    return jax.shard_map(
        on_device,
        mesh=mesh,
        in_specs=(P(None, ("sec", "row"), "col"), P(None, ("sec", "row"), "col")),
        out_specs=(P(None, ("sec", "row"), "col"), P("sec", None)),
        check_vma=False,
    )
```
